256 devices in a mesh: tile: 64 (over x, z, core), lev: 4 (over y).
Axes of the slice: x: 4, y: 4, z: 8, core: 2. Of those that a mesh axis runs over, the one named last changes fastest.
Arguments:
- anomalies: bfloat16 [50, 16, 1152, 384], P(None, 'lev', 'tile'), may hold values from -6 to 6
- lanczos: bfloat16 [100, 16, 1152, 384], P(None, 'lev', 'tile'), may hold values from -6 to 6
- eigen_weight: float32 [100], replicated, may hold values from 0.02 to 0.3
- stencil_index: int32 [6, 49152], P(None, 'tile'), may hold values from 0 to 9215, as said below
- stencil_weight: float32 [6, 49152], P(None, 'tile'), may hold values from 0.05 to 0.35
- member_slot: int32 [50], replicated, may hold values from 0 to 63, as said below
Outputs:
- updated: bfloat16 [50, 16, 1152, 384], P(None, 'lev', 'tile')
- owned: bfloat16 [64, 16, 384, 128], P('tile', 'lev')
The draws below stay inside these ranges and needn't reach their ends.
Inputs may be any that keep to these rules, and one draw needn't show every extreme that they name: `stencil_index`: positions within a block of 24 x 384. `member_slot`: distinct for distinct members; slot s belongs to tile s.
All inputs are finite; a program needn't handle non-finite values.
Results may differ from the reference program's by a relative error of at most 0.0065.
Values may be sent and summed in bfloat16 or wider, within the bound.
A program may use at most 128 MiB of HBM per device.

```python
import math
import jax
import jax.numpy as jnp
from jax import lax

VECTORS = 100
MEMBERS = 50
HY = 18
HX = 384
POINTS = 6
CY = 6
CX = 128
COARSE_DEV = 768
NCOARSE = 49152
LEVELS = 16
NY = 1152
CELLS = 7077888
SLOTS = 64
N_TILE = 64


def draw_stencil_index(key, part):
    key = jax.random.fold_in(key, 11)
    key_rows, key_cols = jax.random.split(key)
    shift_row = jax.random.randint(key_rows, (POINTS, NCOARSE), -4, 5)
    shift_col = jax.random.randint(key_cols, (POINTS, NCOARSE), -1, 2)
    point = jnp.arange(POINTS)[:, None]
    shift_row = jnp.where(point == 0, -4, jnp.where(point == POINTS - 1, 4, shift_row))
    shift_col = jnp.where(point == 0, -1, jnp.where(point == POINTS - 1, 1, shift_col))
    cell = jnp.arange(NCOARSE) % COARSE_DEV
    coarse_row = cell // CX
    coarse_col = cell % CX
    row = 3 * coarse_row[None, :] + 4 + shift_row
    col = 3 * coarse_col[None, :] + 1 + shift_col
    return (row * HX + col).astype(jnp.int32)


def draw_member_slot(key, part):
    key = jax.random.fold_in(key, 23)
    key_pick, key_order = jax.random.split(key)
    middle = jax.random.permutation(key_pick, SLOTS - 2)[:MEMBERS - 2] + 1
    values = jnp.concatenate([jnp.array([0, SLOTS - 1]), middle])
    return jax.random.permutation(key_order, values).astype(jnp.int32)


def levels(key, shape, cuts, low, top_value):
    def one(position, shards_of):
        steps = jax.random.uniform(jax.random.fold_in(jax.random.fold_in(key, 6), position), (shards_of,), jnp.float32, low / len(cuts), top_value / len(cuts))
        return jnp.repeat(jnp.exp(steps), shape[position] // shards_of).reshape((-1,) + (1,) * (len(shape) - position - 1))

    factor_of = one(*cuts[0])
    for cut in cuts[1:]:
        factor_of = factor_of * one(*cut)
    return factor_of


def bell_draw(own_key, shape, scale, bound, cuts=(), held_as=jnp.bfloat16):
    values = jax.random.normal(own_key, shape, jnp.float32) * scale
    if len(cuts) > 0:
        values = levels(own_key, shape, cuts, -0.22, 0.18) * values
    return jnp.clip(values, min=-bound, max=bound).astype(held_as)


def setup_inputs(seed: int = 0) -> dict:
    key_list = jax.random.split(jax.random.key(seed), 7)
    anomalies = bell_draw(key_list[0], (MEMBERS, LEVELS, NY, HX), 1.0, 6.0, ((1, 4), (2, 64)))
    lanczos = bell_draw(key_list[1], (VECTORS, LEVELS, NY, HX), 1.0, 6.0, ((1, 4), (2, 64)))
    eigen_weight = jnp.clip(jnp.exp(jax.random.uniform(key_list[2], (VECTORS,), jnp.float32, math.log(0.02), math.log(0.3))), 0.02, 0.3)
    stencil_index = draw_stencil_index(jax.random.fold_in(key_list[6], 71), 0)
    stencil_weight = jnp.clip(0.05 + 0.29999999 * jax.random.uniform(key_list[4], (POINTS, NCOARSE), jnp.float32) ** levels(key_list[4], (POINTS, NCOARSE), ((1, 64),), -0.2, 0.2), 0.05, 0.35)
    member_slot = draw_member_slot(jax.random.fold_in(key_list[6], 71), 0)
    return dict(anomalies=anomalies, lanczos=lanczos, eigen_weight=eigen_weight, stencil_index=stencil_index, stencil_weight=stencil_weight, member_slot=member_slot)


def reference(anomalies, lanczos, eigen_weight, stencil_index, stencil_weight, member_slot):
    flat_x = anomalies.reshape(MEMBERS, -1)
    flat_v = lanczos.reshape(VECTORS, -1)
    projection = lax.dot_general(flat_v, flat_x, (((1,), (1,)), ((), ())), preferred_element_type=jnp.float32)
    coefficients = (eigen_weight[:, None] * projection / math.sqrt(CELLS)).astype(jnp.bfloat16)
    increment = lax.dot_general(coefficients, flat_v, (((0,), (0,)), ((), ())), preferred_element_type=jnp.float32)
    updated = (flat_x - increment).astype(jnp.bfloat16).reshape(anomalies.shape)
    padded = jnp.pad(updated, ((0, 0), (0, 0), (3, 3), (0, 0)))

    def one_tile(tile_no):
        block = lax.dynamic_slice_in_dim(padded, (tile_no * HY).astype(jnp.int32), HY + 6, 2)
        block = block.reshape(MEMBERS * LEVELS, -1)
        start = (tile_no * COARSE_DEV).astype(jnp.int32)
        index_part = lax.dynamic_slice_in_dim(stencil_index, start, COARSE_DEV, 1)
        weight_part = lax.dynamic_slice_in_dim(stencil_weight, start, COARSE_DEV, 1)
        picked = jnp.take(block, index_part.reshape(-1), axis=1).reshape(MEMBERS * LEVELS, POINTS, COARSE_DEV)
        return (picked.astype(jnp.float32) * weight_part[None]).sum(1).astype(jnp.bfloat16)
    pieces = lax.map(one_tile, jnp.arange(N_TILE, dtype=jnp.int32))
    pieces = pieces.reshape(N_TILE, MEMBERS, LEVELS, CY, CX)
    restricted = jnp.transpose(pieces, (1, 2, 0, 3, 4)).reshape(MEMBERS, -1)
    selector = (member_slot[None, :] == jnp.arange(SLOTS, dtype=jnp.int32)[:, None]).astype(jnp.bfloat16)
    owned = jnp.dot(selector, restricted, preferred_element_type=jnp.float32).astype(jnp.bfloat16)
    return (updated, owned.reshape(SLOTS, LEVELS, CY * N_TILE, CX))
```

```python
import functools
import math

import jax
import jax.numpy as jnp
from jax import lax
from jax.experimental import pallas as pl
from jax.experimental.pallas import tpu as pltpu
from jax.sharding import PartitionSpec as P

BF = jnp.bfloat16
F32 = jnp.float32
I32 = jnp.int32
MESH = pl.DeviceIdType.MESH

MEMBERS, VECTORS, LEV, ROWS, COLS = 50, 100, 4, 18, 384
POINTS, CELLS = 6, 768
HALO = 3
CB = COLS // 128
OWN = ROWS * CB
SIDE = HALO * CB
NB = OWN + 2 * SIDE
ML, KL = MEMBERS * LEV, VECTORS * LEV
SLOTS = 64
WAVES = 3
PM, PK = 64, 128


def iota(shape, dim):
    return lax.broadcasted_iota(I32, shape, dim)


def dot(a, b):
    return lax.dot_general(a, b, (((1,), (0,)), ((), ())), preferred_element_type=F32)


def one_hot(cond):
    return jnp.where(cond, 1.0, 0.0).astype(BF)


def split3(a):
    hi = a.astype(BF)
    rest = a - hi.astype(F32)
    mid = rest.astype(BF)
    return hi, mid, (rest - mid.astype(F32)).astype(BF)


def lanes(ref, first, count):
    return jnp.concatenate([ref[first + i] for i in range(count)], axis=1)


def prepare_stencil(idx, wgt, off, blk, wts):
    rows = [idx[p : p + 1, :] for p in range(POINTS)]
    weights = [wgt[p : p + 1, :] for p in range(POINTS)]
    for p in range(POINTS):
        moved = None
        for q in range(p + 1, POINTS):
            same = rows[p] == rows[q]
            hit = same if moved is None else same & ~moved
            weights[q] = jnp.where(hit, weights[q] + weights[p], weights[q])
            moved = same if moved is None else moved | same
        block = rows[p] >> 7
        blk[p : p + 1, :] = block if moved is None else jnp.where(moved, -1, block)
        off[p : p + 1, :] = rows[p] & 127
        wts[p : p + 1, :] = weights[p]


def build_stencil(off, blk, wts, sten, first, last):
    for c in range(CELLS // 128):
        cs = slice(c * 128, (c + 1) * 128)
        weights = [jnp.broadcast_to(wts[p : p + 1, cs], (16, 128)).astype(BF) for p in range(POINTS)]
        places = [(iota((16, 128), 0) + 16 * i).astype(F32).astype(BF) for i in range(8)]
        blocks, offsets = blk[:, cs], off[:, cs]

        def body(b, carry):
            local = jnp.where(blocks == b, offsets, -1).astype(F32)
            here = [jnp.broadcast_to(local[p : p + 1, :], (16, 128)).astype(BF) for p in range(POINTS)]
            for i in range(8):
                value = jnp.zeros((16, 128), BF)
                for p in range(POINTS):
                    value = jnp.where(here[p] == places[i], weights[p], value)
                sten[b, i * 16 : (i + 1) * 16, cs] = value
            return carry

        lax.fori_loop(first, last, body, 0)


def kernel(
    tiles, levs, g1, cells_total,
    x, v, idx, wgt, eig, slot,
    upd, own,
    xs, vs, us, lo, hi, sten, acc, off, blk, wts, part, ra, rb, rc, mine, ms,
    load_sem, out_sem, ar_send, ar_recv, halo_send, halo_recv, a2a_send, a2a_recv, self_sem,
):
    tile, lev = lax.axis_index("tile"), lax.axis_index("lev")
    g2t = tiles // g1
    g2 = g2t * levs
    member1 = lax.rem(tile, g1)
    group1 = tile // g1
    member2 = group1 * levs + lev

    chunks = 3
    per = ROWS // chunks

    def load_row(r, carry):
        k = r // per
        for c in range(CB):
            cols = pl.ds(c * 128, 128)
            pltpu.make_async_copy(x.at[:, r, :, cols], xs.at[r * CB + c], load_sem.at[k]).start()
            pltpu.make_async_copy(v.at[:, r, :, cols], vs.at[r * CB + c], load_sem.at[chunks + k]).start()
        return carry

    lax.fori_loop(0, ROWS, load_row, 0)

    barrier = pltpu.get_barrier_semaphore()

    def greet(d, carry):
        pl.semaphore_signal(
            barrier, inc=1, device_id={"tile": lax.rem(tile + d, tiles)}, device_id_type=MESH
        )
        return carry

    lax.fori_loop(1, tiles, greet, 0)

    def greet_lev(d, carry):
        e, q = d // g2t + 1, lax.rem(d, g2t)
        pl.semaphore_signal(
            barrier, inc=1,
            device_id={"tile": q * g1 + member1, "lev": lax.rem(lev + e, levs)},
            device_id_type=MESH,
        )
        return carry

    lax.fori_loop(0, (levs - 1) * g2t, greet_lev, 0)

    prepare_stencil(idx, wgt, off, blk, wts)
    build_stencil(off, blk, wts, sten, 0, NB)

    xf = xs.reshape(OWN, ML, 128)
    vf = vs.reshape(OWN, KL, 128)
    uf = us.reshape(OWN, ML, 128)
    step = OWN // chunks
    gram = None
    for k in range(chunks):
        here = pl.ds(k * step, step)
        pltpu.make_async_copy(xs.at[here], xs.at[here], load_sem.at[k]).wait()
        pltpu.make_async_copy(vs.at[here], vs.at[here], load_sem.at[chunks + k]).wait()
        term = lax.dot_general(
            lanes(xf, k * step, step), lanes(vf, k * step, step),
            (((1,), (1,)), ((), ())), preferred_element_type=F32,
        )
        gram = term if gram is None else gram + term
    same_lev = (iota((ML, KL), 0) & 3) == (iota((ML, KL), 1) & 3)
    gram = jnp.where(same_lev, gram, 0.0)
    fold_m = one_hot((iota((PM, ML), 1) >> 2) == iota((PM, ML), 0))
    fold_k = one_hot((iota((KL, PK), 0) >> 2) == iota((KL, PK), 1))
    folded = sum(dot(fold_m, piece) for piece in split3(gram))
    partial = sum(dot(piece, fold_k) for piece in split3(folded))
    sh = PM // g1
    part.reshape(PM, PK)[...] = partial

    pl.semaphore_wait(barrier, tiles - 1 + (levs - 1) * g2t)

    def send_a(d, carry):
        to = lax.rem(member1 + d, g1)
        pltpu.make_async_remote_copy(
            src_ref=part.at[to], dst_ref=ra.at[member1], send_sem=ar_send.at[0], recv_sem=ar_recv.at[0],
            device_id={"tile": group1 * g1 + to}, device_id_type=MESH,
        ).start()
        return carry

    lax.fori_loop(1, g1, send_a, 0)
    ra[member1] = part[member1]
    pltpu.make_async_copy(ra.at[pl.ds(0, g1 - 1)], ra.at[pl.ds(0, g1 - 1)], ar_recv.at[0]).wait()
    total = ra[0]
    for i in range(1, g1):
        total = total + ra[i]
    mine[0] = total

    def send_b(d, carry):
        to = lax.rem(member2 + d, g2)
        pltpu.make_async_remote_copy(
            src_ref=mine.at[0], dst_ref=rb.at[member2], send_sem=ar_send.at[1], recv_sem=ar_recv.at[1],
            device_id={"tile": (to // levs) * g1 + member1, "lev": lax.rem(to, levs)}, device_id_type=MESH,
        ).start()
        return carry

    lax.fori_loop(1, g2, send_b, 0)
    rb[member2] = total
    pltpu.make_async_copy(rb.at[pl.ds(0, g2 - 1)], rb.at[pl.ds(0, g2 - 1)], ar_recv.at[1]).wait()
    total = rb[0]
    for i in range(1, g2):
        total = total + rb[i]
    mine[1] = total

    def send_c(d, carry):
        to = lax.rem(member1 + d, g1)
        pltpu.make_async_remote_copy(
            src_ref=mine.at[1], dst_ref=rc.at[member1], send_sem=ar_send.at[2], recv_sem=ar_recv.at[2],
            device_id={"tile": group1 * g1 + to}, device_id_type=MESH,
        ).start()
        return carry

    lax.fori_loop(1, g1, send_c, 0)
    rc[member1] = total

    spread_m = one_hot((iota((ML, PM), 0) >> 2) == iota((ML, PM), 1))
    spread_k = one_hot((iota((PK, KL), 1) >> 2) == iota((PK, KL), 0))
    slot_row = jnp.broadcast_to(slot[...], (8, MEMBERS)).astype(F32).astype(BF)
    spread_slot = one_hot((iota((MEMBERS, ML), 1) >> 2) == iota((MEMBERS, ML), 0))
    slot_ml = dot(slot_row, spread_slot)[0:1, :].astype(I32)
    out_rows = SLOTS * LEV * 2
    row, col = iota((out_rows, ML), 0), iota((out_rows, ML), 1)
    taken = ((row >> 3) == slot_ml) & (((row >> 1) & 3) == (col & 3))
    select = [one_hot(taken & ((row & 1) == r)) for r in range(2)]

    pltpu.make_async_copy(rc.at[pl.ds(0, g1 - 1)], rc.at[pl.ds(0, g1 - 1)], ar_recv.at[2]).wait()
    projection = rc.reshape(PM, PK)[...]
    eig_row = jnp.concatenate([eig[...], jnp.zeros((1, PK - VECTORS), F32)], axis=1)
    coef = (eig_row * projection / math.sqrt(cells_total)).astype(BF)
    coef = dot(dot(spread_m, coef).astype(BF), spread_k)
    coef = jnp.where(same_lev, coef, 0.0).astype(BF)

    def update(first, count):
        inc = dot(coef, lanes(vf, first, count))
        for i in range(count):
            uf[first + i] = (
                xf[first + i].astype(F32) - inc[:, i * 128 : (i + 1) * 128]
            ).astype(BF)

    def halo_copy(first, dst, k, to):
        return pltpu.make_async_remote_copy(
            src_ref=us.at[pl.ds(first, SIDE)], dst_ref=dst, send_sem=halo_send.at[k],
            recv_sem=halo_recv.at[k], device_id={"tile": to}, device_id_type=MESH,
        )

    to_low = halo_copy(0, hi, 0, lax.rem(tile + tiles - 1, tiles))
    to_high = halo_copy(OWN - SIDE, lo, 1, lax.rem(tile + 1, tiles))
    update(0, SIDE)
    pl.when(tile > 0)(lambda: to_low.start())
    update(OWN - SIDE, SIDE)
    pl.when(tile < tiles - 1)(lambda: to_high.start())
    for i in range(2):
        update(SIDE + 18 * i, 18)

    def store_row(r, carry):
        for c in range(CB):
            pltpu.make_async_copy(us.at[r * CB + c], upd.at[:, r, :, pl.ds(c * 128, 128)], out_sem).start()
        return carry

    lax.fori_loop(0, ROWS, store_row, 0)

    acc[...] = dot(lanes(uf, 0, OWN), sten[pl.ds(SIDE, OWN)].reshape(OWN * 128, CELLS))

    @pl.when(tile == 0)
    def _():
        lo[...] = jnp.zeros_like(lo)

    @pl.when(tile == tiles - 1)
    def _():
        hi[...] = jnp.zeros_like(hi)

    pl.when(tile < tiles - 1)(lambda: to_low.wait_recv())
    pl.when(tile > 0)(lambda: to_high.wait_recv())

    wave_cells = CELLS // WAVES
    both = jnp.concatenate(
        [lanes(lo.reshape(SIDE, ML, 128), 0, SIDE), lanes(hi.reshape(SIDE, ML, 128), 0, SIDE)], axis=1
    )
    msf = ms.reshape(WAVES, out_rows, 128)
    for j in range(WAVES):
        cs = slice(j * wave_cells, (j + 1) * wave_cells)
        edge = jnp.concatenate(
            [
                sten[pl.ds(0, SIDE), :, cs].reshape(SIDE * 128, wave_cells),
                sten[pl.ds(SIDE + OWN, SIDE), :, cs].reshape(SIDE * 128, wave_cells),
            ],
            axis=0,
        )
        res = (acc[:, cs] + dot(both, edge)).astype(BF)
        msf[j] = (dot(select[0], res[:, :128]) + dot(select[1], res[:, 128:])).astype(BF)

        def send(d, carry):
            to = lax.rem(tile + d, tiles)
            pltpu.make_async_remote_copy(
                src_ref=ms.at[j, to], dst_ref=own.at[:, tile * WAVES + j], send_sem=a2a_send.at[j],
                recv_sem=a2a_recv, device_id={"tile": to}, device_id_type=MESH,
            ).start()
            return carry

        lax.fori_loop(1, tiles, send, 0)
        pltpu.make_async_copy(ms.at[j, tile], own.at[:, tile * WAVES + j], self_sem.at[j]).start()

    for k, n in ((0, g1), (1, g2), (2, g1)):
        pltpu.make_async_copy(ra.at[pl.ds(0, n - 1)], ra.at[pl.ds(0, n - 1)], ar_send.at[k]).wait()
    pl.when(tile > 0)(lambda: to_low.wait_send())
    pl.when(tile < tiles - 1)(lambda: to_high.wait_send())
    pltpu.make_async_copy(us, us, out_sem).wait()
    for j in range(WAVES):
        pltpu.make_async_copy(ms.at[j, tile], own.at[:, tile * WAVES + j], self_sem.at[j]).wait()
        others = ms.at[j, pl.ds(0, tiles - 1)]
        pltpu.make_async_copy(others, others, a2a_send.at[j]).wait()
    others = own.at[:, pl.ds(0, (tiles - 1) * WAVES)]
    pltpu.make_async_copy(others, others, a2a_recv).wait()


def shards(anomalies, lanczos, eigen_weight, stencil_index, stencil_weight, member_slot):
    tiles, levs = lax.axis_size("tile"), lax.axis_size("lev")
    g1 = min(16, tiles)
    g2 = tiles // g1 * levs
    sh = PM // g1
    total = LEV * ROWS * COLS * tiles * levs
    hbm = pl.BlockSpec(memory_space=pltpu.HBM)
    vmem = pl.BlockSpec(memory_space=pltpu.VMEM)
    updated, owned = pl.pallas_call(
        functools.partial(kernel, tiles, levs, g1, total),
        out_shape=(
            jax.ShapeDtypeStruct((MEMBERS, ROWS, LEV, COLS), BF),
            jax.ShapeDtypeStruct((LEV, tiles * WAVES, 2, 128), BF),
        ),
        in_specs=[hbm, hbm, vmem, vmem, vmem, vmem],
        out_specs=(hbm, hbm),
        scratch_shapes=[
            pltpu.VMEM((OWN, MEMBERS, LEV, 128), BF),
            pltpu.VMEM((OWN, VECTORS, LEV, 128), BF),
            pltpu.VMEM((OWN, MEMBERS, LEV, 128), BF),
            pltpu.VMEM((SIDE, MEMBERS, LEV, 128), BF),
            pltpu.VMEM((SIDE, MEMBERS, LEV, 128), BF),
            pltpu.VMEM((NB, 128, CELLS), BF),
            pltpu.VMEM((ML, CELLS), F32),
            pltpu.VMEM((POINTS, CELLS), I32),
            pltpu.VMEM((POINTS, CELLS), I32),
            pltpu.VMEM((POINTS, CELLS), F32),
            pltpu.VMEM((g1, sh, PK), F32),
            pltpu.VMEM((g1, sh, PK), F32),
            pltpu.VMEM((g2, sh, PK), F32),
            pltpu.VMEM((g1, sh, PK), F32),
            pltpu.VMEM((2, sh, PK), F32),
            pltpu.VMEM((WAVES, SLOTS, LEV, 2, 128), BF),
            pltpu.SemaphoreType.DMA((6,)),
            pltpu.SemaphoreType.DMA(()),
            pltpu.SemaphoreType.DMA((3,)),
            pltpu.SemaphoreType.DMA((3,)),
            pltpu.SemaphoreType.DMA((2,)),
            pltpu.SemaphoreType.DMA((2,)),
            pltpu.SemaphoreType.DMA((WAVES,)),
            pltpu.SemaphoreType.DMA(()),
            pltpu.SemaphoreType.DMA((WAVES,)),
        ],
        compiler_params=pltpu.CompilerParams(
            collective_id=0, has_side_effects=True, vmem_limit_bytes=56 * 2**20
        ),
    )(
        anomalies.transpose(0, 2, 1, 3),
        lanczos.transpose(0, 2, 1, 3),
        stencil_index,
        stencil_weight,
        eigen_weight.reshape(1, -1),
        member_slot.reshape(1, -1),
    )
    return updated.transpose(0, 2, 1, 3), owned.reshape(1, LEV, tiles * 6, 128)


def solution(mesh):
    placed = (
        P(None, "lev", "tile", None),
        P(None, "lev", "tile", None),
        P(),
        P(None, "tile"),
        P(None, "tile"),
        P(),
    )
    return jax.shard_map(
        shards,
        mesh=mesh,
        in_specs=placed,
        out_specs=(P(None, "lev", "tile", None), P("tile", "lev", None, None)),
        check_vma=False,
    )
```

```python
import functools
import math

import jax
import jax.numpy as jnp
from jax import lax
from jax.experimental import pallas as pl
from jax.experimental.pallas import tpu as pltpu
from jax.sharding import PartitionSpec as P

BF = jnp.bfloat16
F32 = jnp.float32
I32 = jnp.int32
MESH = pl.DeviceIdType.MESH

MEMBERS, VECTORS, LEV, ROWS, COLS = 50, 100, 4, 18, 384
POINTS, CELLS = 6, 768
HALO = 3
CB = COLS // 128
OWN = ROWS * CB
SIDE = HALO * CB
NB = OWN + 2 * SIDE
ML, KL = MEMBERS * LEV, VECTORS * LEV
SLOTS = 64
WAVES = 3
BUILD = ((0, 10), (10, 15), (15, 20), (20, 46), (46, NB))
PM, PK = 64, 128


def iota(shape, dim):
    return lax.broadcasted_iota(I32, shape, dim)


def dot(a, b):
    return lax.dot_general(a, b, (((1,), (0,)), ((), ())), preferred_element_type=F32)


def one_hot(cond):
    return jnp.where(cond, 1.0, 0.0).astype(BF)


def split3(a):
    hi = a.astype(BF)
    rest = a - hi.astype(F32)
    mid = rest.astype(BF)
    return hi, mid, (rest - mid.astype(F32)).astype(BF)


def lanes(ref, first, count):
    return jnp.concatenate([ref[first + i] for i in range(count)], axis=1)


def far_first(i, n):
    half, sign = (i + 1) // 2, 1 - 2 * lax.rem(i, 2)
    return lax.rem(n // 2 + sign * half + n, n)


def prepare_stencil(idx, wgt, off, blk, wts):
    rows = [idx[p : p + 1, :] for p in range(POINTS)]
    weights = [wgt[p : p + 1, :] for p in range(POINTS)]
    for p in range(POINTS):
        moved = None
        for q in range(p + 1, POINTS):
            same = rows[p] == rows[q]
            hit = same if moved is None else same & ~moved
            weights[q] = jnp.where(hit, weights[q] + weights[p], weights[q])
            moved = same if moved is None else moved | same
        block = rows[p] >> 7
        blk[p : p + 1, :] = block if moved is None else jnp.where(moved, -1, block)
        off[p : p + 1, :] = rows[p] & 127
        wts[p : p + 1, :] = weights[p]


def build_stencil(off, blk, wts, sten, first, last):
    for c in range(CELLS // 128):
        cs = slice(c * 128, (c + 1) * 128)
        weights = [jnp.broadcast_to(wts[p : p + 1, cs], (16, 128)).astype(BF) for p in range(POINTS)]
        places = [(iota((16, 128), 0) + 16 * i).astype(F32).astype(BF) for i in range(8)]
        blocks, offsets = blk[:, cs], off[:, cs]

        def body(b, carry):
            local = jnp.where(blocks == b, offsets, -1).astype(F32)
            here = [jnp.broadcast_to(local[p : p + 1, :], (16, 128)).astype(BF) for p in range(POINTS)]
            for i in range(8):
                value = jnp.zeros((16, 128), BF)
                for p in range(POINTS):
                    value = jnp.where(here[p] == places[i], weights[p], value)
                sten[b, i * 16 : (i + 1) * 16, cs] = value
            return carry

        lax.fori_loop(first, last, body, 0)


def kernel(
    tiles, levs, grid, cells_total,
    x, v, idx_in, wgt_in, eig_in, slot_in,
    upd, own,
    idx, wgt, eig, slot, small_sem, xs, vs, us, lo, hi, sten, acc, off, blk, wts, part, ra, rb, rc, sums, ms,
    load_sem, out_sem, ar_send, ar_recv, halo_send, halo_recv, a2a_send, a2a_recv, self_sem,
):
    tile, lev = lax.axis_index("tile"), lax.axis_index("lev")
    nx, nz, nc = grid
    row_len = nz * nc
    my_x, my_zc = tile // row_len, lax.rem(tile, row_len)
    my_z, my_c = my_zc // nc, lax.rem(my_zc, nc)
    n1, n2 = nx * levs, nz * nc
    mine1, mine2 = my_x * levs + lev, my_zc

    def peer1(i):
        to_x = lax.rem(my_x + far_first(i // levs, nx), nx)
        to_lev = lax.rem(lev + far_first(lax.rem(i, levs), levs), levs)
        return to_x * levs + to_lev, {"tile": to_x * row_len + my_zc, "lev": to_lev}

    def peer2(i):
        to_z = lax.rem(my_z + far_first(i // nc, nz), nz)
        to_c = lax.rem(my_c + far_first(lax.rem(i, nc), nc), nc)
        return to_z * nc + to_c, {"tile": my_x * row_len + to_z * nc + to_c}

    def peer_tile(i):
        to_z = lax.rem(my_z + far_first(i // (nx * nc), nz), nz)
        to_x = lax.rem(my_x + far_first(lax.rem(i // nc, nx), nx), nx)
        to_c = lax.rem(my_c + far_first(lax.rem(i, nc), nc), nc)
        return to_x * row_len + to_z * nc + to_c

    chunks = 3
    per = ROWS // chunks

    def load_row(r, carry):
        k = r // per
        for c in range(CB):
            cols = pl.ds(c * 128, 128)
            pltpu.make_async_copy(x.at[:, r, :, cols], xs.at[r * CB + c], load_sem.at[k]).start()
            pltpu.make_async_copy(v.at[:, r, :, cols], vs.at[r * CB + c], load_sem.at[chunks + k]).start()
        return carry

    smalls = [
        pltpu.make_async_copy(src, dst, small_sem.at[i])
        for i, (src, dst) in enumerate(((idx_in, idx), (wgt_in, wgt), (eig_in, eig), (slot_in, slot)))
    ]
    for copy in smalls:
        copy.start()
    lax.fori_loop(0, ROWS, load_row, 0)

    barrier = pltpu.get_barrier_semaphore()

    def greet(i, carry):
        pl.semaphore_signal(barrier, inc=1, device_id={"tile": peer_tile(i)}, device_id_type=MESH)
        return carry

    def greet_lev(i, carry):
        to = {
            "tile": i // (levs - 1) * row_len + my_zc,
            "lev": lax.rem(lev + 1 + lax.rem(i, levs - 1), levs),
        }
        pl.semaphore_signal(barrier, inc=1, device_id=to, device_id_type=MESH)
        return carry

    lax.fori_loop(0, tiles - 1, greet, 0)
    if levs > 1:
        lax.fori_loop(0, nx * (levs - 1), greet_lev, 0)

    for copy in smalls:
        copy.wait()
    prepare_stencil(idx, wgt, off, blk, wts)

    xf = xs.reshape(OWN, ML, 128)
    vf = vs.reshape(OWN, KL, 128)
    uf = us.reshape(OWN, ML, 128)
    step = OWN // chunks
    gram = None
    for k in range(chunks):
        build_stencil(off, blk, wts, sten, *BUILD[k])
        here = pl.ds(k * step, step)
        pltpu.make_async_copy(xs.at[here], xs.at[here], load_sem.at[k]).wait()
        pltpu.make_async_copy(vs.at[here], vs.at[here], load_sem.at[chunks + k]).wait()
        term = lax.dot_general(
            lanes(xf, k * step, step), lanes(vf, k * step, step),
            (((1,), (1,)), ((), ())), preferred_element_type=F32,
        )
        gram = term if gram is None else gram + term
    same_lev = (iota((ML, KL), 0) & 3) == (iota((ML, KL), 1) & 3)
    gram = jnp.where(same_lev, gram, 0.0)
    fold_m = one_hot((iota((PM, ML), 1) >> 2) == iota((PM, ML), 0))
    fold_k = one_hot((iota((KL, PK), 0) >> 2) == iota((KL, PK), 1))
    folded = sum(dot(fold_m, piece) for piece in split3(gram))
    partial = sum(dot(piece, fold_k) for piece in split3(folded))
    part.reshape(PM, PK)[...] = partial

    pl.semaphore_wait(barrier, tiles - 1 + nx * (levs - 1))

    def ar_stage(k, n, peer, src, dst, mine):
        def send(i, carry):
            to, device = peer(i)
            pltpu.make_async_remote_copy(
                src_ref=src(to), dst_ref=dst.at[mine], send_sem=ar_send.at[k], recv_sem=ar_recv.at[k],
                device_id=device, device_id_type=MESH,
            ).start()
            return carry

        lax.fori_loop(0, n - 1, send, 0)

    def ar_wait(k, n, dst):
        got = dst.at[pl.ds(0, n - 1)]
        pltpu.make_async_copy(got, got, ar_recv.at[k]).wait()

    def add_up(ref, n):
        terms = [ref[i] for i in range(n)]
        while len(terms) > 1:
            terms = [a + b for a, b in zip(terms[::2], terms[1::2])]
        return terms[0]

    ar_stage(0, n1, peer1, lambda to: part.at[to], ra, mine1)
    ra[mine1] = part[mine1]
    build_stencil(off, blk, wts, sten, *BUILD[3])
    ar_wait(0, n1, ra)
    total = add_up(ra, n1)
    sums[0] = total
    ar_stage(1, n2, peer2, lambda to: sums.at[0], rb, mine2)
    rb[mine2] = total
    build_stencil(off, blk, wts, sten, *BUILD[4])
    ar_wait(1, n2, rb)
    total = add_up(rb, n2)
    sums[1] = total
    ar_stage(2, n1, peer1, lambda to: sums.at[1], rc, mine1)
    rc[mine1] = total

    spread_m = one_hot((iota((ML, PM), 0) >> 2) == iota((ML, PM), 1))
    spread_k = one_hot((iota((PK, KL), 1) >> 2) == iota((PK, KL), 0))
    slot_row = jnp.broadcast_to(slot[...], (8, MEMBERS)).astype(F32).astype(BF)
    spread_slot = one_hot((iota((MEMBERS, ML), 1) >> 2) == iota((MEMBERS, ML), 0))
    slot_ml = dot(slot_row, spread_slot)[0:1, :].astype(I32)
    out_rows = SLOTS * LEV * 2
    row, col = iota((out_rows, ML), 0), iota((out_rows, ML), 1)
    taken = ((row >> 3) == slot_ml) & (((row >> 1) & 3) == (col & 3))
    select = [one_hot(taken & ((row & 1) == r)) for r in range(2)]

    ar_wait(2, n1, rc)
    projection = rc.reshape(PM, PK)[...]
    eig_row = jnp.concatenate([eig[...], jnp.zeros((1, PK - VECTORS), F32)], axis=1)
    coef = (eig_row * projection / math.sqrt(cells_total)).astype(BF)
    coef = dot(dot(spread_m, coef).astype(BF), spread_k)
    coef = jnp.where(same_lev, coef, 0.0).astype(BF)

    def update(first, count):
        inc = dot(coef, lanes(vf, first, count))
        for i in range(count):
            uf[first + i] = (
                xf[first + i].astype(F32) - inc[:, i * 128 : (i + 1) * 128]
            ).astype(BF)

    def halo_copy(first, dst, k, to):
        return pltpu.make_async_remote_copy(
            src_ref=us.at[pl.ds(first, SIDE)], dst_ref=dst, send_sem=halo_send.at[k],
            recv_sem=halo_recv.at[k], device_id={"tile": to}, device_id_type=MESH,
        )

    to_low = halo_copy(0, hi, 0, lax.rem(tile + tiles - 1, tiles))
    to_high = halo_copy(OWN - SIDE, lo, 1, lax.rem(tile + 1, tiles))
    update(0, SIDE)
    pl.when(tile > 0)(lambda: to_low.start())
    update(OWN - SIDE, SIDE)
    pl.when(tile < tiles - 1)(lambda: to_high.start())
    for i in range(2):
        update(SIDE + 18 * i, 18)

    def store_row(r, carry):
        for c in range(CB):
            pltpu.make_async_copy(us.at[r * CB + c], upd.at[:, r, :, pl.ds(c * 128, 128)], out_sem).start()
        return carry

    lax.fori_loop(0, ROWS, store_row, 0)

    acc[...] = dot(lanes(uf, 0, OWN), sten[pl.ds(SIDE, OWN)].reshape(OWN * 128, CELLS))

    @pl.when(tile == 0)
    def _():
        lo[...] = jnp.zeros_like(lo)

    @pl.when(tile == tiles - 1)
    def _():
        hi[...] = jnp.zeros_like(hi)

    pl.when(tile < tiles - 1)(lambda: to_low.wait_recv())
    pl.when(tile > 0)(lambda: to_high.wait_recv())

    wave_cells = CELLS // WAVES
    both = jnp.concatenate(
        [lanes(lo.reshape(SIDE, ML, 128), 0, SIDE), lanes(hi.reshape(SIDE, ML, 128), 0, SIDE)], axis=1
    )
    msf = ms.reshape(WAVES, out_rows, 128)
    for j in range(WAVES):
        cs = slice(j * wave_cells, (j + 1) * wave_cells)
        edge = jnp.concatenate(
            [
                sten[pl.ds(0, SIDE), :, cs].reshape(SIDE * 128, wave_cells),
                sten[pl.ds(SIDE + OWN, SIDE), :, cs].reshape(SIDE * 128, wave_cells),
            ],
            axis=0,
        )
        res = (acc[:, cs] + dot(both, edge)).astype(BF)
        msf[j] = (dot(select[0], res[:, :128]) + dot(select[1], res[:, 128:])).astype(BF)

        def send(i, carry):
            to = peer_tile(i)
            pltpu.make_async_remote_copy(
                src_ref=ms.at[j, to], dst_ref=own.at[:, tile * WAVES + j], send_sem=a2a_send.at[j],
                recv_sem=a2a_recv, device_id={"tile": to}, device_id_type=MESH,
            ).start()
            return carry

        lax.fori_loop(0, tiles - 1, send, 0)
        pltpu.make_async_copy(ms.at[j, tile], own.at[:, tile * WAVES + j], self_sem.at[j]).start()

    for k, n, dst in ((0, n1, ra), (1, n2, rb), (2, n1, rc)):
        sent = dst.at[pl.ds(0, n - 1)]
        pltpu.make_async_copy(sent, sent, ar_send.at[k]).wait()
    pl.when(tile > 0)(lambda: to_low.wait_send())
    pl.when(tile < tiles - 1)(lambda: to_high.wait_send())
    pltpu.make_async_copy(us, us, out_sem).wait()
    for j in range(WAVES):
        pltpu.make_async_copy(ms.at[j, tile], own.at[:, tile * WAVES + j], self_sem.at[j]).wait()
        others = ms.at[j, pl.ds(0, tiles - 1)]
        pltpu.make_async_copy(others, others, a2a_send.at[j]).wait()
    others = own.at[:, pl.ds(0, (tiles - 1) * WAVES)]
    pltpu.make_async_copy(others, others, a2a_recv).wait()


def deliver(a, b, upd, own, sem):
    copies = [pltpu.make_async_copy(a, upd, sem.at[0]), pltpu.make_async_copy(b, own, sem.at[1])]
    for copy in copies:
        copy.start()
    for copy in copies:
        copy.wait()


def shards(anomalies, lanczos, eigen_weight, stencil_index, stencil_weight, member_slot):
    tiles, levs = lax.axis_size("tile"), lax.axis_size("lev")
    grid = (4, 8, 2) if tiles == 64 else (1, 1, tiles)
    n1, n2 = grid[0] * levs, grid[1] * grid[2]
    sh = PM // n1
    total = LEV * ROWS * COLS * tiles * levs
    hbm = pl.BlockSpec(memory_space=pltpu.HBM)
    shapes = (
        jax.ShapeDtypeStruct((MEMBERS, ROWS, LEV, COLS), BF),
        jax.ShapeDtypeStruct((LEV, tiles * WAVES, 2, 128), BF),
    )
    anywhere = pl.BlockSpec(memory_space=pl.ANY)
    updated, owned = pl.pallas_call(
        functools.partial(kernel, tiles, levs, grid, total),
        out_shape=shapes,
        in_specs=[hbm] * 6,
        out_specs=(anywhere, anywhere),
        scratch_shapes=[
            pltpu.VMEM((POINTS, CELLS), I32),
            pltpu.VMEM((POINTS, CELLS), F32),
            pltpu.VMEM((1, VECTORS), F32),
            pltpu.VMEM((1, MEMBERS), I32),
            pltpu.SemaphoreType.DMA((4,)),
            pltpu.VMEM((OWN, MEMBERS, LEV, 128), BF),
            pltpu.VMEM((OWN, VECTORS, LEV, 128), BF),
            pltpu.VMEM((OWN, MEMBERS, LEV, 128), BF),
            pltpu.VMEM((SIDE, MEMBERS, LEV, 128), BF),
            pltpu.VMEM((SIDE, MEMBERS, LEV, 128), BF),
            pltpu.VMEM((NB, 128, CELLS), BF),
            pltpu.VMEM((ML, CELLS), F32),
            pltpu.VMEM((POINTS, CELLS), I32),
            pltpu.VMEM((POINTS, CELLS), I32),
            pltpu.VMEM((POINTS, CELLS), F32),
            pltpu.VMEM((n1, sh, PK), F32),
            pltpu.VMEM((n1, sh, PK), F32),
            pltpu.VMEM((n2, sh, PK), F32),
            pltpu.VMEM((n1, sh, PK), F32),
            pltpu.VMEM((2, sh, PK), F32),
            pltpu.VMEM((WAVES, SLOTS, LEV, 2, 128), BF),
            pltpu.SemaphoreType.DMA((6,)),
            pltpu.SemaphoreType.DMA(()),
            pltpu.SemaphoreType.DMA((3,)),
            pltpu.SemaphoreType.DMA((3,)),
            pltpu.SemaphoreType.DMA((2,)),
            pltpu.SemaphoreType.DMA((2,)),
            pltpu.SemaphoreType.DMA((WAVES,)),
            pltpu.SemaphoreType.DMA(()),
            pltpu.SemaphoreType.DMA((WAVES,)),
        ],
        compiler_params=pltpu.CompilerParams(
            collective_id=0, has_side_effects=True, vmem_limit_bytes=36 * 2**20
        ),
    )(
        *(
            pltpu.with_memory_space_constraint(a, pltpu.HBM)
            for a in (
                anomalies.transpose(0, 2, 1, 3),
                lanczos.transpose(0, 2, 1, 3),
                stencil_index,
                stencil_weight,
                eigen_weight.reshape(1, -1),
                member_slot.reshape(1, -1),
            )
        )
    )
    updated, owned = pl.pallas_call(
        deliver,
        out_shape=shapes,
        in_specs=[anywhere, anywhere],
        out_specs=(hbm, hbm),
        scratch_shapes=[pltpu.SemaphoreType.DMA((2,))],
        compiler_params=pltpu.CompilerParams(vmem_limit_bytes=2**20),
    )(updated, owned)
    return updated.transpose(0, 2, 1, 3), owned.reshape(1, LEV, tiles * 6, 128)


def solution(mesh):
    placed = (
        P(None, "lev", "tile", None),
        P(None, "lev", "tile", None),
        P(),
        P(None, "tile"),
        P(None, "tile"),
        P(),
    )
    return jax.shard_map(
        shards,
        mesh=mesh,
        in_specs=placed,
        out_specs=(P(None, "lev", "tile", None), P("tile", "lev", None, None)),
        check_vma=False,
    )
```

```python
import functools
import math

import jax
import jax.numpy as jnp
from jax import lax
from jax.experimental import pallas as pl
from jax.experimental.pallas import tpu as pltpu
from jax.sharding import PartitionSpec as P

BF = jnp.bfloat16
F32 = jnp.float32
I32 = jnp.int32
MESH = pl.DeviceIdType.MESH

MEMBERS, VECTORS, LEV, ROWS, COLS = 50, 100, 4, 18, 384
POINTS, CELLS = 6, 768
HALO = 3
CB = COLS // 128
OWN = ROWS * CB
SIDE = HALO * CB
NB = OWN + 2 * SIDE
ML, KL = MEMBERS * LEV, VECTORS * LEV
SLOTS = 64
WAVES = 3
BUILD = ((0, 10), (10, 15), (15, 20), (20, 46), (46, NB))
PM, PK = 64, 128


def iota(shape, dim):
    return lax.broadcasted_iota(I32, shape, dim)


def dot(a, b):
    return lax.dot_general(a, b, (((1,), (0,)), ((), ())), preferred_element_type=F32)


def one_hot(cond):
    return jnp.where(cond, 1.0, 0.0).astype(BF)


def split3(a):
    hi = a.astype(BF)
    rest = a - hi.astype(F32)
    mid = rest.astype(BF)
    return hi, mid, (rest - mid.astype(F32)).astype(BF)


def lanes(ref, first, count):
    return jnp.concatenate([ref[first + i] for i in range(count)], axis=1)


def far_first(i, n):
    half, sign = (i + 1) // 2, 1 - 2 * lax.rem(i, 2)
    return lax.rem(n // 2 + sign * half + n, n)


def prepare_stencil(idx, wgt, off, blk, wts):
    rows = [idx[p : p + 1, :] for p in range(POINTS)]
    weights = [wgt[p : p + 1, :] for p in range(POINTS)]
    for p in range(POINTS):
        moved = None
        for q in range(p + 1, POINTS):
            same = rows[p] == rows[q]
            hit = same if moved is None else same & ~moved
            weights[q] = jnp.where(hit, weights[q] + weights[p], weights[q])
            moved = same if moved is None else moved | same
        block = rows[p] >> 7
        blk[p : p + 1, :] = block if moved is None else jnp.where(moved, -1, block)
        off[p : p + 1, :] = rows[p] & 127
        wts[p : p + 1, :] = weights[p]


def build_stencil(off, blk, wts, sten, first, last):
    for c in range(CELLS // 128):
        cs = slice(c * 128, (c + 1) * 128)
        weights = [jnp.broadcast_to(wts[p : p + 1, cs], (16, 128)).astype(BF) for p in range(POINTS)]
        places = [(iota((16, 128), 0) + 16 * i).astype(F32).astype(BF) for i in range(8)]
        blocks, offsets = blk[:, cs], off[:, cs]

        def body(b, carry):
            local = jnp.where(blocks == b, offsets, -1).astype(F32)
            here = [jnp.broadcast_to(local[p : p + 1, :], (16, 128)).astype(BF) for p in range(POINTS)]
            for i in range(8):
                value = jnp.zeros((16, 128), BF)
                for p in range(POINTS):
                    value = jnp.where(here[p] == places[i], weights[p], value)
                sten[b, i * 16 : (i + 1) * 16, cs] = value
            return carry

        lax.fori_loop(first, last, body, 0)


def kernel(
    tiles, levs, grid, cells_total,
    x, v, idx_in, wgt_in, eig_in, slot_in,
    upd, own,
    idx, wgt, eig, slot, small_sem, xs, vs, us, sten, off, blk, wts, part, ra, rb, rc, sums, ms,
    load_sem, out_sem, ar_send, ar_recv, halo_send, halo_recv, a2a_send, a2a_recv, self_sem,
):
    tile, lev = lax.axis_index("tile"), lax.axis_index("lev")
    nx, nz, nc = grid
    row_len = nz * nc
    my_x, my_zc = tile // row_len, lax.rem(tile, row_len)
    my_z, my_c = my_zc // nc, lax.rem(my_zc, nc)
    n1, n2 = nx * levs, nz * nc
    mine1, mine2 = my_x * levs + lev, my_zc

    def peer1(i):
        to_x = lax.rem(my_x + far_first(i // levs, nx), nx)
        to_lev = lax.rem(lev + far_first(lax.rem(i, levs), levs), levs)
        return to_x * levs + to_lev, {"tile": to_x * row_len + my_zc, "lev": to_lev}

    def peer2(i):
        to_z = lax.rem(my_z + far_first(i // nc, nz), nz)
        to_c = lax.rem(my_c + far_first(lax.rem(i, nc), nc), nc)
        return to_z * nc + to_c, {"tile": my_x * row_len + to_z * nc + to_c}

    def peer_tile(i):
        to_z = lax.rem(my_z + far_first(i // (nx * nc), nz), nz)
        to_x = lax.rem(my_x + far_first(lax.rem(i // nc, nx), nx), nx)
        to_c = lax.rem(my_c + far_first(lax.rem(i, nc), nc), nc)
        return to_x * row_len + to_z * nc + to_c

    chunks = 3
    per = ROWS // chunks

    def load_row(r, carry):
        k = r // per
        for c in range(CB):
            cols = pl.ds(c * 128, 128)
            b = SIDE + r * CB + c
            pltpu.make_async_copy(x.at[:, r, :, cols], xs.at[b], load_sem.at[k]).start()
            pltpu.make_async_copy(v.at[:, r, :, cols], vs.at[b], load_sem.at[chunks + k]).start()
        return carry

    smalls = [
        pltpu.make_async_copy(src, dst, small_sem.at[i])
        for i, (src, dst) in enumerate(((idx_in, idx), (wgt_in, wgt), (eig_in, eig), (slot_in, slot)))
    ]
    for copy in smalls:
        copy.start()
    lax.fori_loop(0, ROWS, load_row, 0)

    barrier = pltpu.get_barrier_semaphore()

    def greet(i, carry):
        pl.semaphore_signal(barrier, inc=1, device_id={"tile": peer_tile(i)}, device_id_type=MESH)
        return carry

    def greet_lev(i, carry):
        to = {
            "tile": i // (levs - 1) * row_len + my_zc,
            "lev": lax.rem(lev + 1 + lax.rem(i, levs - 1), levs),
        }
        pl.semaphore_signal(barrier, inc=1, device_id=to, device_id_type=MESH)
        return carry

    lax.fori_loop(0, tiles - 1, greet, 0)
    if levs > 1:
        lax.fori_loop(0, nx * (levs - 1), greet_lev, 0)

    for copy in smalls:
        copy.wait()
    prepare_stencil(idx, wgt, off, blk, wts)

    xf = xs.reshape(NB, ML, 128)
    vf = vs.reshape(NB, KL, 128)
    uf = us.reshape(NB, ML, 128)
    step = OWN // chunks
    gram = None
    for k in range(chunks):
        build_stencil(off, blk, wts, sten, *BUILD[k])
        first = SIDE + k * step
        here = pl.ds(first, step)
        pltpu.make_async_copy(xs.at[here], xs.at[here], load_sem.at[k]).wait()
        pltpu.make_async_copy(vs.at[here], vs.at[here], load_sem.at[chunks + k]).wait()
        term = lax.dot_general(
            lanes(xf, first, step), lanes(vf, first, step),
            (((1,), (1,)), ((), ())), preferred_element_type=F32,
        )
        gram = term if gram is None else gram + term
    same_lev = (iota((ML, KL), 0) & 3) == (iota((ML, KL), 1) & 3)
    gram = jnp.where(same_lev, gram, 0.0)
    fold_m = one_hot((iota((PM, ML), 1) >> 2) == iota((PM, ML), 0))
    fold_k = one_hot((iota((KL, PK), 0) >> 2) == iota((KL, PK), 1))
    folded = sum(dot(fold_m, piece) for piece in split3(gram))
    partial = sum(dot(piece, fold_k) for piece in split3(folded))
    part.reshape(PM, PK)[...] = partial

    pl.semaphore_wait(barrier, tiles - 1 + nx * (levs - 1))

    def halo_copy(ref, first, dst, k, to):
        return pltpu.make_async_remote_copy(
            src_ref=ref.at[pl.ds(first, SIDE)], dst_ref=ref.at[pl.ds(dst, SIDE)], send_sem=halo_send.at[k],
            recv_sem=halo_recv.at[k], device_id={"tile": to}, device_id_type=MESH,
        )

    down, up = lax.rem(tile + tiles - 1, tiles), lax.rem(tile + 1, tiles)
    to_low = [halo_copy(ref, SIDE, SIDE + OWN, k, down) for k, ref in enumerate((xs, vs))]
    to_high = [halo_copy(ref, OWN, 0, 2 + k, up) for k, ref in enumerate((xs, vs))]

    @pl.when(tile > 0)
    def _():
        for copy in to_low:
            copy.start()

    @pl.when(tile < tiles - 1)
    def _():
        for copy in to_high:
            copy.start()

    @pl.when(tile == 0)
    def _():
        for ref in (xs, vs):
            ref[pl.ds(0, SIDE)] = jnp.zeros((SIDE,) + ref.shape[1:], BF)

    @pl.when(tile == tiles - 1)
    def _():
        for ref in (xs, vs):
            ref[pl.ds(SIDE + OWN, SIDE)] = jnp.zeros((SIDE,) + ref.shape[1:], BF)

    def ar_stage(k, n, peer, src, dst, mine):
        def send(i, carry):
            to, device = peer(i)
            pltpu.make_async_remote_copy(
                src_ref=src(to), dst_ref=dst.at[mine], send_sem=ar_send.at[k], recv_sem=ar_recv.at[k],
                device_id=device, device_id_type=MESH,
            ).start()
            return carry

        lax.fori_loop(0, n - 1, send, 0)

    def ar_wait(k, n, dst):
        got = dst.at[pl.ds(0, n - 1)]
        pltpu.make_async_copy(got, got, ar_recv.at[k]).wait()

    def add_up(ref, n):
        terms = [ref[i] for i in range(n)]
        while len(terms) > 1:
            terms = [a + b for a, b in zip(terms[::2], terms[1::2])]
        return terms[0]

    ar_stage(0, n1, peer1, lambda to: part.at[to], ra, mine1)
    ra[mine1] = part[mine1]
    build_stencil(off, blk, wts, sten, *BUILD[3])
    ar_wait(0, n1, ra)
    total = add_up(ra, n1)
    sums[0] = total
    ar_stage(1, n2, peer2, lambda to: sums.at[0], rb, mine2)
    rb[mine2] = total
    build_stencil(off, blk, wts, sten, *BUILD[4])
    ar_wait(1, n2, rb)
    total = add_up(rb, n2)
    sums[1] = total
    ar_stage(2, n1, peer1, lambda to: sums.at[1], rc, mine1)
    rc[mine1] = total

    spread_m = one_hot((iota((ML, PM), 0) >> 2) == iota((ML, PM), 1))
    spread_k = one_hot((iota((PK, KL), 1) >> 2) == iota((PK, KL), 0))
    slot_row = jnp.broadcast_to(slot[...], (8, MEMBERS)).astype(F32).astype(BF)
    spread_slot = one_hot((iota((MEMBERS, ML), 1) >> 2) == iota((MEMBERS, ML), 0))
    slot_ml = dot(slot_row, spread_slot)[0:1, :].astype(I32)
    out_rows = SLOTS * LEV * 2
    row, col = iota((out_rows, ML), 0), iota((out_rows, ML), 1)
    taken = ((row >> 3) == slot_ml) & (((row >> 1) & 3) == (col & 3))
    select = [one_hot(taken & ((row & 1) == r)) for r in range(2)]

    ar_wait(2, n1, rc)
    projection = rc.reshape(PM, PK)[...]
    eig_row = jnp.concatenate([eig[...], jnp.zeros((1, PK - VECTORS), F32)], axis=1)
    coef = (eig_row * projection / math.sqrt(cells_total)).astype(BF)
    coef = dot(dot(spread_m, coef).astype(BF), spread_k)
    coef = jnp.where(same_lev, coef, 0.0).astype(BF)

    def update(first, count):
        inc = dot(coef, lanes(vf, first, count))
        for i in range(count):
            uf[first + i] = (
                xf[first + i].astype(F32) - inc[:, i * 128 : (i + 1) * 128]
            ).astype(BF)

    for i in range(chunks):
        update(SIDE + step * i, step)

    def store_row(r, carry):
        for c in range(CB):
            pltpu.make_async_copy(
                us.at[SIDE + r * CB + c], upd.at[:, r, :, pl.ds(c * 128, 128)], out_sem
            ).start()
        return carry

    lax.fori_loop(0, ROWS, store_row, 0)

    @pl.when(tile < tiles - 1)
    def _():
        for copy in to_low:
            copy.wait_recv()

    @pl.when(tile > 0)
    def _():
        for copy in to_high:
            copy.wait_recv()

    update(0, SIDE)
    update(SIDE + OWN, SIDE)

    wave_cells = CELLS // WAVES
    msf = ms.reshape(WAVES, out_rows, 128)
    for j in range(WAVES):
        cs = slice(j * wave_cells, (j + 1) * wave_cells)
        res = dot(lanes(uf, 0, NB), sten[:, :, cs].reshape(NB * 128, wave_cells)).astype(BF)
        msf[j] = (dot(select[0], res[:, :128]) + dot(select[1], res[:, 128:])).astype(BF)

        def send(i, carry):
            to = peer_tile(i)
            pltpu.make_async_remote_copy(
                src_ref=ms.at[j, to], dst_ref=own.at[:, tile * WAVES + j], send_sem=a2a_send.at[j],
                recv_sem=a2a_recv, device_id={"tile": to}, device_id_type=MESH,
            ).start()
            return carry

        lax.fori_loop(0, tiles - 1, send, 0)
        pltpu.make_async_copy(ms.at[j, tile], own.at[:, tile * WAVES + j], self_sem.at[j]).start()

    for k, n, dst in ((0, n1, ra), (1, n2, rb), (2, n1, rc)):
        sent = dst.at[pl.ds(0, n - 1)]
        pltpu.make_async_copy(sent, sent, ar_send.at[k]).wait()

    @pl.when(tile > 0)
    def _():
        for copy in to_low:
            copy.wait_send()

    @pl.when(tile < tiles - 1)
    def _():
        for copy in to_high:
            copy.wait_send()

    stored = us.at[pl.ds(0, OWN)]
    pltpu.make_async_copy(stored, stored, out_sem).wait()
    for j in range(WAVES):
        pltpu.make_async_copy(ms.at[j, tile], own.at[:, tile * WAVES + j], self_sem.at[j]).wait()
        others = ms.at[j, pl.ds(0, tiles - 1)]
        pltpu.make_async_copy(others, others, a2a_send.at[j]).wait()
    others = own.at[:, pl.ds(0, (tiles - 1) * WAVES)]
    pltpu.make_async_copy(others, others, a2a_recv).wait()


def deliver(a, b, upd, own, sem):
    copies = [pltpu.make_async_copy(a, upd, sem.at[0]), pltpu.make_async_copy(b, own, sem.at[1])]
    for copy in copies:
        copy.start()
    for copy in copies:
        copy.wait()


def shards(anomalies, lanczos, eigen_weight, stencil_index, stencil_weight, member_slot):
    tiles, levs = lax.axis_size("tile"), lax.axis_size("lev")
    grid = (4, 8, 2) if tiles == 64 else (1, 1, tiles)
    n1, n2 = grid[0] * levs, grid[1] * grid[2]
    sh = PM // n1
    total = LEV * ROWS * COLS * tiles * levs
    hbm = pl.BlockSpec(memory_space=pltpu.HBM)
    shapes = (
        jax.ShapeDtypeStruct((MEMBERS, ROWS, LEV, COLS), BF),
        jax.ShapeDtypeStruct((LEV, tiles * WAVES, 2, 128), BF),
    )
    anywhere = pl.BlockSpec(memory_space=pl.ANY)
    updated, owned = pl.pallas_call(
        functools.partial(kernel, tiles, levs, grid, total),
        out_shape=shapes,
        in_specs=[hbm] * 6,
        out_specs=(anywhere, anywhere),
        scratch_shapes=[
            pltpu.VMEM((POINTS, CELLS), I32),
            pltpu.VMEM((POINTS, CELLS), F32),
            pltpu.VMEM((1, VECTORS), F32),
            pltpu.VMEM((1, MEMBERS), I32),
            pltpu.SemaphoreType.DMA((4,)),
            pltpu.VMEM((NB, MEMBERS, LEV, 128), BF),
            pltpu.VMEM((NB, VECTORS, LEV, 128), BF),
            pltpu.VMEM((NB, MEMBERS, LEV, 128), BF),
            pltpu.VMEM((NB, 128, CELLS), BF),
            pltpu.VMEM((POINTS, CELLS), I32),
            pltpu.VMEM((POINTS, CELLS), I32),
            pltpu.VMEM((POINTS, CELLS), F32),
            pltpu.VMEM((n1, sh, PK), F32),
            pltpu.VMEM((n1, sh, PK), F32),
            pltpu.VMEM((n2, sh, PK), F32),
            pltpu.VMEM((n1, sh, PK), F32),
            pltpu.VMEM((2, sh, PK), F32),
            pltpu.VMEM((WAVES, SLOTS, LEV, 2, 128), BF),
            pltpu.SemaphoreType.DMA((6,)),
            pltpu.SemaphoreType.DMA(()),
            pltpu.SemaphoreType.DMA((3,)),
            pltpu.SemaphoreType.DMA((3,)),
            pltpu.SemaphoreType.DMA((4,)),
            pltpu.SemaphoreType.DMA((4,)),
            pltpu.SemaphoreType.DMA((WAVES,)),
            pltpu.SemaphoreType.DMA(()),
            pltpu.SemaphoreType.DMA((WAVES,)),
        ],
        compiler_params=pltpu.CompilerParams(
            collective_id=0, has_side_effects=True, vmem_limit_bytes=40 * 2**20
        ),
    )(
        *(
            pltpu.with_memory_space_constraint(a, pltpu.HBM)
            for a in (
                anomalies.transpose(0, 2, 1, 3),
                lanczos.transpose(0, 2, 1, 3),
                stencil_index,
                stencil_weight,
                eigen_weight.reshape(1, -1),
                member_slot.reshape(1, -1),
            )
        )
    )
    updated, owned = pl.pallas_call(
        deliver,
        out_shape=shapes,
        in_specs=[anywhere, anywhere],
        out_specs=(hbm, hbm),
        scratch_shapes=[pltpu.SemaphoreType.DMA((2,))],
        compiler_params=pltpu.CompilerParams(vmem_limit_bytes=2**20),
    )(updated, owned)
    return updated.transpose(0, 2, 1, 3), owned.reshape(1, LEV, tiles * 6, 128)


def solution(mesh):
    placed = (
        P(None, "lev", "tile", None),
        P(None, "lev", "tile", None),
        P(),
        P(None, "tile"),
        P(None, "tile"),
        P(),
    )
    return jax.shard_map(
        shards,
        mesh=mesh,
        in_specs=placed,
        out_specs=(P(None, "lev", "tile", None), P("tile", "lev", None, None)),
        check_vma=False,
    )
```

```python
import functools
import math

import jax
import jax.numpy as jnp
from jax import lax
from jax.experimental import pallas as pl
from jax.experimental.pallas import tpu as pltpu
from jax.sharding import PartitionSpec as P

BF = jnp.bfloat16
F32 = jnp.float32
I32 = jnp.int32
MESH = pl.DeviceIdType.MESH

MEMBERS, VECTORS, LEV, ROWS, COLS = 50, 100, 4, 18, 384
POINTS, CELLS = 6, 768
HALO = 3
CB = COLS // 128
OWN = ROWS * CB
SIDE = HALO * CB
NB = OWN + 2 * SIDE
ML, KL = MEMBERS * LEV, VECTORS * LEV
SLOTS = 64
WAVES = 3
BUILD = ((0, 10), (10, 15), (15, 20), (20, 46), (46, NB))
PM, PK = 64, 128


def iota(shape, dim):
    return lax.broadcasted_iota(I32, shape, dim)


def dot(a, b):
    return lax.dot_general(a, b, (((1,), (0,)), ((), ())), preferred_element_type=F32)


def one_hot(cond):
    return jnp.where(cond, 1.0, 0.0).astype(BF)


def split3(a):
    hi = a.astype(BF)
    rest = a - hi.astype(F32)
    mid = rest.astype(BF)
    return hi, mid, (rest - mid.astype(F32)).astype(BF)


def lanes(ref, first, count):
    return jnp.concatenate([ref[first + i] for i in range(count)], axis=1)


def far_first(i):
    return ((((0x01627354 >> ((i >> 3) * 4)) & 7) << 1) | (((i >> 1) & 3) << 4) | (i & 1)) ^ 49


def prepare_stencil(idx, wgt, off, blk, wts):
    rows = [idx[p : p + 1, :] for p in range(POINTS)]
    weights = [wgt[p : p + 1, :] for p in range(POINTS)]
    for p in range(POINTS):
        moved = None
        for q in range(p + 1, POINTS):
            same = rows[p] == rows[q]
            hit = same if moved is None else same & ~moved
            weights[q] = jnp.where(hit, weights[q] + weights[p], weights[q])
            moved = same if moved is None else moved | same
        block = rows[p] >> 7
        blk[p : p + 1, :] = block if moved is None else jnp.where(moved, -1, block)
        off[p : p + 1, :] = rows[p] & 127
        wts[p : p + 1, :] = weights[p]


def build_stencil(off, blk, wts, sten, first, last):
    for c in range(CELLS // 128):
        cs = slice(c * 128, (c + 1) * 128)
        weights = [jnp.broadcast_to(wts[p : p + 1, cs], (16, 128)).astype(BF) for p in range(POINTS)]
        places = [(iota((16, 128), 0) + 16 * i).astype(F32).astype(BF) for i in range(8)]
        blocks, offsets = blk[:, cs], off[:, cs]

        def body(b, carry):
            local = jnp.where(blocks == b, offsets, -1).astype(F32)
            here = [jnp.broadcast_to(local[p : p + 1, :], (16, 128)).astype(BF) for p in range(POINTS)]
            for i in range(8):
                value = jnp.zeros((16, 128), BF)
                for p in range(POINTS):
                    value = jnp.where(here[p] == places[i], weights[p], value)
                sten[b, i * 16 : (i + 1) * 16, cs] = value
            return carry

        lax.fori_loop(first, last, body, 0)


def kernel(
    tiles, levs, grid, cells_total,
    x, v, idx_in, wgt_in, eig_in, slot_in,
    upd, own,
    idx, wgt, eig, slot, small_sem, xs, vs, us, lo, hi, sten, acc, off, blk, wts, part, ra, rb, rc, sums, ms,
    load_sem, out_sem, ar_send, ar_recv, halo_send, halo_recv, a2a_send, a2a_recv, self_sem,
):
    tile, lev = lax.axis_index("tile"), lax.axis_index("lev")
    nx, nz, nc = grid
    row_len = nz * nc
    my_x, my_zc = tile // row_len, lax.rem(tile, row_len)
    n1, n2 = nx * levs, nz * nc
    mine1, mine2 = my_x * levs + lev, my_zc
    lev_bits = levs.bit_length() - 1

    def peer1(i):
        to = mine1 ^ i
        return to, {"tile": (to >> lev_bits) * row_len + my_zc, "lev": to & (levs - 1)}

    def peer2(i):
        return mine2 ^ i, {"tile": tile ^ i}

    chunks = 3
    per = ROWS // chunks

    def load_row(r, carry):
        k = r // per
        for c in range(CB):
            cols = pl.ds(c * 128, 128)
            pltpu.make_async_copy(x.at[:, r, :, cols], xs.at[r * CB + c], load_sem.at[k]).start()
            pltpu.make_async_copy(v.at[:, r, :, cols], vs.at[r * CB + c], load_sem.at[chunks + k]).start()
        return carry

    smalls = [
        pltpu.make_async_copy(src, dst, small_sem.at[i])
        for i, (src, dst) in enumerate(((idx_in, idx), (wgt_in, wgt), (eig_in, eig), (slot_in, slot)))
    ]
    for copy in smalls:
        copy.start()
    lax.fori_loop(0, ROWS, load_row, 0)

    barrier = pltpu.get_barrier_semaphore()

    def greet(i, carry):
        pl.semaphore_signal(barrier, inc=1, device_id={"tile": tile ^ i}, device_id_type=MESH)
        return carry

    lax.fori_loop(1, tiles, greet, 0)
    for e in range(1, levs):
        for q in range(nx):
            to = {"tile": tile ^ (q * row_len), "lev": lev ^ e}
            pl.semaphore_signal(barrier, inc=1, device_id=to, device_id_type=MESH)

    for copy in smalls:
        copy.wait()
    prepare_stencil(idx, wgt, off, blk, wts)

    xf = xs.reshape(OWN, ML, 128)
    vf = vs.reshape(OWN, KL, 128)
    uf = us.reshape(OWN, ML, 128)
    step = OWN // chunks
    gram = None
    for k in range(chunks):
        build_stencil(off, blk, wts, sten, *BUILD[k])
        here = pl.ds(k * step, step)
        pltpu.make_async_copy(xs.at[here], xs.at[here], load_sem.at[k]).wait()
        pltpu.make_async_copy(vs.at[here], vs.at[here], load_sem.at[chunks + k]).wait()
        term = lax.dot_general(
            lanes(xf, k * step, step), lanes(vf, k * step, step),
            (((1,), (1,)), ((), ())), preferred_element_type=F32,
        )
        gram = term if gram is None else gram + term
    same_lev = (iota((ML, KL), 0) & 3) == (iota((ML, KL), 1) & 3)
    gram = jnp.where(same_lev, gram, 0.0)
    fold_m = one_hot((iota((PM, ML), 1) >> 2) == iota((PM, ML), 0))
    fold_k = one_hot((iota((KL, PK), 0) >> 2) == iota((KL, PK), 1))
    folded = sum(dot(fold_m, piece) for piece in split3(gram))
    partial = sum(dot(piece, fold_k) for piece in split3(folded))
    part.reshape(PM, PK)[...] = partial

    pl.semaphore_wait(barrier, tiles - 1 + nx * (levs - 1))

    def ar_stage(k, n, peer, src, dst, mine):
        def send(i, carry):
            to, device = peer(i)
            pltpu.make_async_remote_copy(
                src_ref=src(to), dst_ref=dst.at[mine], send_sem=ar_send.at[k], recv_sem=ar_recv.at[k],
                device_id=device, device_id_type=MESH,
            ).start()
            return carry

        lax.fori_loop(1, n, send, 0)

    def ar_wait(k, n, dst):
        got = dst.at[pl.ds(0, n - 1)]
        pltpu.make_async_copy(got, got, ar_recv.at[k]).wait()

    def add_up(ref, n):
        terms = [ref[i] for i in range(n)]
        while len(terms) > 1:
            terms = [a + b for a, b in zip(terms[::2], terms[1::2])]
        return terms[0]

    ar_stage(0, n1, peer1, lambda to: part.at[to], ra, mine1)
    ra[mine1] = part[mine1]
    build_stencil(off, blk, wts, sten, *BUILD[3])
    ar_wait(0, n1, ra)
    total = add_up(ra, n1)
    sums[0] = total
    ar_stage(1, n2, peer2, lambda to: sums.at[0], rb, mine2)
    rb[mine2] = total
    build_stencil(off, blk, wts, sten, *BUILD[4])
    ar_wait(1, n2, rb)
    total = add_up(rb, n2)
    sums[1] = total
    ar_stage(2, n1, peer1, lambda to: sums.at[1], rc, mine1)
    rc[mine1] = total

    spread_m = one_hot((iota((ML, PM), 0) >> 2) == iota((ML, PM), 1))
    spread_k = one_hot((iota((PK, KL), 1) >> 2) == iota((PK, KL), 0))
    slot_row = jnp.broadcast_to(slot[...], (8, MEMBERS)).astype(F32).astype(BF)
    spread_slot = one_hot((iota((MEMBERS, ML), 1) >> 2) == iota((MEMBERS, ML), 0))
    slot_ml = dot(slot_row, spread_slot)[0:1, :].astype(I32)
    out_rows = SLOTS * LEV * 2
    row, col = iota((out_rows, ML), 0), iota((out_rows, ML), 1)
    taken = ((row >> 3) == slot_ml) & (((row >> 1) & 3) == (col & 3))
    select = [one_hot(taken & ((row & 1) == r)) for r in range(2)]

    ar_wait(2, n1, rc)
    projection = rc.reshape(PM, PK)[...]
    eig_row = jnp.concatenate([eig[...], jnp.zeros((1, PK - VECTORS), F32)], axis=1)
    coef = (eig_row * projection / math.sqrt(cells_total)).astype(BF)
    coef = dot(dot(spread_m, coef).astype(BF), spread_k)
    coef = jnp.where(same_lev, coef, 0.0).astype(BF)

    def update(first, count):
        inc = dot(coef, lanes(vf, first, count))
        for i in range(count):
            uf[first + i] = (
                xf[first + i].astype(F32) - inc[:, i * 128 : (i + 1) * 128]
            ).astype(BF)

    def halo_copy(first, dst, k, to):
        return pltpu.make_async_remote_copy(
            src_ref=us.at[pl.ds(first, SIDE)], dst_ref=dst, send_sem=halo_send.at[k],
            recv_sem=halo_recv.at[k], device_id={"tile": to}, device_id_type=MESH,
        )

    to_low = halo_copy(0, hi, 0, lax.rem(tile + tiles - 1, tiles))
    to_high = halo_copy(OWN - SIDE, lo, 1, lax.rem(tile + 1, tiles))
    update(0, SIDE)
    pl.when(tile > 0)(lambda: to_low.start())
    update(OWN - SIDE, SIDE)
    pl.when(tile < tiles - 1)(lambda: to_high.start())
    for i in range(2):
        update(SIDE + 18 * i, 18)

    def store_row(r, carry):
        for c in range(CB):
            pltpu.make_async_copy(us.at[r * CB + c], upd.at[:, r, :, pl.ds(c * 128, 128)], out_sem).start()
        return carry

    lax.fori_loop(0, ROWS, store_row, 0)

    acc[...] = dot(lanes(uf, 0, OWN), sten[pl.ds(SIDE, OWN)].reshape(OWN * 128, CELLS))

    @pl.when(tile == 0)
    def _():
        lo[...] = jnp.zeros_like(lo)

    @pl.when(tile == tiles - 1)
    def _():
        hi[...] = jnp.zeros_like(hi)

    pl.when(tile < tiles - 1)(lambda: to_low.wait_recv())
    pl.when(tile > 0)(lambda: to_high.wait_recv())

    wave_cells = CELLS // WAVES
    both = jnp.concatenate(
        [lanes(lo.reshape(SIDE, ML, 128), 0, SIDE), lanes(hi.reshape(SIDE, ML, 128), 0, SIDE)], axis=1
    )
    msf = ms.reshape(SLOTS, WAVES, LEV * 2, 128)
    for j in range(WAVES):
        cs = slice(j * wave_cells, (j + 1) * wave_cells)
        edge = jnp.concatenate(
            [
                sten[pl.ds(0, SIDE), :, cs].reshape(SIDE * 128, wave_cells),
                sten[pl.ds(SIDE + OWN, SIDE), :, cs].reshape(SIDE * 128, wave_cells),
            ],
            axis=0,
        )
        res = (acc[:, cs] + dot(both, edge)).astype(BF)
        picked = dot(select[0], res[:, :128]) + dot(select[1], res[:, 128:])
        msf[:, j] = picked.astype(BF).reshape(SLOTS, LEV * 2, 128)

    def send(i, carry):
        to = tile ^ far_first(i)
        pltpu.make_async_remote_copy(
            src_ref=ms.at[to], dst_ref=own.at[tile], send_sem=a2a_send, recv_sem=a2a_recv,
            device_id={"tile": to}, device_id_type=MESH,
        ).start()
        return carry

    lax.fori_loop(0, tiles - 1, send, 0)
    keep = pltpu.make_async_copy(ms.at[tile], own.at[tile], self_sem)
    keep.start()

    for k, n, dst in ((0, n1, ra), (1, n2, rb), (2, n1, rc)):
        sent = dst.at[pl.ds(0, n - 1)]
        pltpu.make_async_copy(sent, sent, ar_send.at[k]).wait()
    pl.when(tile > 0)(lambda: to_low.wait_send())
    pl.when(tile < tiles - 1)(lambda: to_high.wait_send())
    pltpu.make_async_copy(us, us, out_sem).wait()
    keep.wait()
    if tiles > 1:
        others = ms.at[pl.ds(0, tiles - 1)]
        pltpu.make_async_copy(others, others, a2a_send).wait()
        pltpu.make_async_copy(others, others, a2a_recv).wait()


def deliver(a, b, upd, own, sem):
    copies = [pltpu.make_async_copy(a, upd, sem.at[0])]
    for j in range(WAVES):
        for lev in range(LEV):
            k = 1 + j * LEV + lev
            copies.append(pltpu.make_async_copy(b.at[:, j, lev], own.at[lev, :, j], sem.at[k]))
    for copy in copies:
        copy.start()
    for copy in copies:
        copy.wait()


def shards(anomalies, lanczos, eigen_weight, stencil_index, stencil_weight, member_slot):
    tiles, levs = lax.axis_size("tile"), lax.axis_size("lev")
    grid = (4, 8, 2) if tiles == 64 else (1, 1, tiles)
    n1, n2 = grid[0] * levs, grid[1] * grid[2]
    sh = PM // n1
    total = LEV * ROWS * COLS * tiles * levs
    hbm = pl.BlockSpec(memory_space=pltpu.HBM)
    shapes = (
        jax.ShapeDtypeStruct((MEMBERS, ROWS, LEV, COLS), BF),
        jax.ShapeDtypeStruct((tiles, WAVES, LEV, 2, 128), BF),
    )
    final = (shapes[0], jax.ShapeDtypeStruct((LEV, tiles, WAVES, 2, 128), BF))
    anywhere = pl.BlockSpec(memory_space=pl.ANY)
    updated, owned = pl.pallas_call(
        functools.partial(kernel, tiles, levs, grid, total),
        out_shape=shapes,
        in_specs=[hbm] * 6,
        out_specs=(anywhere, anywhere),
        scratch_shapes=[
            pltpu.VMEM((POINTS, CELLS), I32),
            pltpu.VMEM((POINTS, CELLS), F32),
            pltpu.VMEM((1, VECTORS), F32),
            pltpu.VMEM((1, MEMBERS), I32),
            pltpu.SemaphoreType.DMA((4,)),
            pltpu.VMEM((OWN, MEMBERS, LEV, 128), BF),
            pltpu.VMEM((OWN, VECTORS, LEV, 128), BF),
            pltpu.VMEM((OWN, MEMBERS, LEV, 128), BF),
            pltpu.VMEM((SIDE, MEMBERS, LEV, 128), BF),
            pltpu.VMEM((SIDE, MEMBERS, LEV, 128), BF),
            pltpu.VMEM((NB, 128, CELLS), BF),
            pltpu.VMEM((ML, CELLS), F32),
            pltpu.VMEM((POINTS, CELLS), I32),
            pltpu.VMEM((POINTS, CELLS), I32),
            pltpu.VMEM((POINTS, CELLS), F32),
            pltpu.VMEM((n1, sh, PK), F32),
            pltpu.VMEM((n1, sh, PK), F32),
            pltpu.VMEM((n2, sh, PK), F32),
            pltpu.VMEM((n1, sh, PK), F32),
            pltpu.VMEM((2, sh, PK), F32),
            pltpu.VMEM((SLOTS, WAVES, LEV, 2, 128), BF),
            pltpu.SemaphoreType.DMA((6,)),
            pltpu.SemaphoreType.DMA(()),
            pltpu.SemaphoreType.DMA((3,)),
            pltpu.SemaphoreType.DMA((3,)),
            pltpu.SemaphoreType.DMA((2,)),
            pltpu.SemaphoreType.DMA((2,)),
            pltpu.SemaphoreType.DMA(()),
            pltpu.SemaphoreType.DMA(()),
            pltpu.SemaphoreType.DMA(()),
        ],
        compiler_params=pltpu.CompilerParams(
            collective_id=0, has_side_effects=True, vmem_limit_bytes=36 * 2**20
        ),
    )(
        *(
            pltpu.with_memory_space_constraint(a, pltpu.HBM)
            for a in (
                anomalies.transpose(0, 2, 1, 3),
                lanczos.transpose(0, 2, 1, 3),
                stencil_index,
                stencil_weight,
                eigen_weight.reshape(1, -1),
                member_slot.reshape(1, -1),
            )
        )
    )
    updated, owned = pl.pallas_call(
        deliver,
        out_shape=final,
        in_specs=[anywhere, anywhere],
        out_specs=(hbm, hbm),
        scratch_shapes=[pltpu.SemaphoreType.DMA((1 + WAVES * LEV,))],
        compiler_params=pltpu.CompilerParams(vmem_limit_bytes=2**20),
    )(updated, owned)
    return updated.transpose(0, 2, 1, 3), owned.reshape(1, LEV, tiles * 6, 128)


def solution(mesh):
    placed = (
        P(None, "lev", "tile", None),
        P(None, "lev", "tile", None),
        P(),
        P(None, "tile"),
        P(None, "tile"),
        P(),
    )
    return jax.shard_map(
        shards,
        mesh=mesh,
        in_specs=placed,
        out_specs=(P(None, "lev", "tile", None), P("tile", "lev", None, None)),
        check_vma=False,
    )
```

```python
import functools
import math

import jax
import jax.numpy as jnp
from jax import lax
from jax.experimental import pallas as pl
from jax.experimental.pallas import tpu as pltpu
from jax.sharding import PartitionSpec as P

BF = jnp.bfloat16
F32 = jnp.float32
I32 = jnp.int32
MESH = pl.DeviceIdType.MESH

MEMBERS, VECTORS, LEV, ROWS, COLS = 50, 100, 4, 18, 384
POINTS, CELLS = 6, 768
HALO = 3
CB = COLS // 128
OWN = ROWS * CB
SIDE = HALO * CB
NB = OWN + 2 * SIDE
ML, KL = MEMBERS * LEV, VECTORS * LEV
SLOTS = 64
WAVES = 3
BUILD = ((9, 18), (18, 23), (23, 28), (28, 63))
PM, PK = 64, 128


def iota(shape, dim):
    return lax.broadcasted_iota(I32, shape, dim)


def dot(a, b):
    return lax.dot_general(a, b, (((1,), (0,)), ((), ())), preferred_element_type=F32)


def one_hot(cond):
    return jnp.where(cond, 1.0, 0.0).astype(BF)


def split3(a):
    hi = a.astype(BF)
    rest = a - hi.astype(F32)
    mid = rest.astype(BF)
    return hi, mid, (rest - mid.astype(F32)).astype(BF)


def lanes(ref, first, count):
    return jnp.concatenate([ref[first + i] for i in range(count)], axis=1)


def far_first(i):
    return ((((0x01627354 >> ((i >> 3) * 4)) & 7) << 1) | (((i >> 1) & 3) << 4) | (i & 1)) ^ 49


def prepare_stencil(idx, wgt, off, blk, wts):
    rows = [idx[p : p + 1, :] for p in range(POINTS)]
    weights = [wgt[p : p + 1, :] for p in range(POINTS)]
    for p in range(POINTS):
        moved = None
        for q in range(p + 1, POINTS):
            same = rows[p] == rows[q]
            hit = same if moved is None else same & ~moved
            weights[q] = jnp.where(hit, weights[q] + weights[p], weights[q])
            moved = same if moved is None else moved | same
        block = rows[p] >> 7
        blk[p : p + 1, :] = block if moved is None else jnp.where(moved, -1, block)
        off[p : p + 1, :] = rows[p] & 127
        wts[p : p + 1, :] = weights[p]


def build_stencil(off, blk, wts, sten, first, last):
    for c in range(CELLS // 128):
        cs = slice(c * 128, (c + 1) * 128)
        weights = [jnp.broadcast_to(wts[p : p + 1, cs], (16, 128)).astype(BF) for p in range(POINTS)]
        places = [(iota((16, 128), 0) + 16 * i).astype(F32).astype(BF) for i in range(8)]
        blocks, offsets = blk[:, cs], off[:, cs]

        def body(b, carry):
            local = jnp.where(blocks == b, offsets, -1).astype(F32)
            here = [jnp.broadcast_to(local[p : p + 1, :], (16, 128)).astype(BF) for p in range(POINTS)]
            for i in range(8):
                value = jnp.zeros((16, 128), BF)
                for p in range(POINTS):
                    value = jnp.where(here[p] == places[i], weights[p], value)
                sten[b, i * 16 : (i + 1) * 16, cs] = value
            return carry

        lax.fori_loop(first, last, body, 0)


def kernel(
    tiles, levs, grid, cells_total,
    x, v, idx_in, wgt_in, eig_in, slot_in,
    upd, own,
    idx, wgt, eig, slot, small_sem, xs, vs, us, lo, hi, sten, rx, rv, off, blk, wts, part, ra, rb, rc, sums, ms,
    load_sem, out_sem, ar_send, ar_recv, halo_send, halo_recv, a2a_send, a2a_recv, self_sem,
):
    tile, lev = lax.axis_index("tile"), lax.axis_index("lev")
    nx, nz, nc = grid
    row_len = nz * nc
    my_x, my_zc = tile // row_len, lax.rem(tile, row_len)
    n1, n2 = nx * levs, nz * nc
    mine1, mine2 = my_x * levs + lev, my_zc
    lev_bits = levs.bit_length() - 1

    def peer1(i):
        to = mine1 ^ i
        return to, {"tile": (to >> lev_bits) * row_len + my_zc, "lev": to & (levs - 1)}

    def peer2(i):
        return mine2 ^ i, {"tile": tile ^ i}

    chunks = 3
    per = ROWS // chunks

    def load_row(r, carry):
        k = r // per
        for c in range(CB):
            cols = pl.ds(c * 128, 128)
            pltpu.make_async_copy(x.at[:, r, :, cols], xs.at[r * CB + c], load_sem.at[k]).start()
            pltpu.make_async_copy(v.at[:, r, :, cols], vs.at[r * CB + c], load_sem.at[chunks + k]).start()
        return carry

    smalls = [
        pltpu.make_async_copy(src, dst, small_sem.at[i])
        for i, (src, dst) in enumerate(((idx_in, idx), (wgt_in, wgt), (eig_in, eig), (slot_in, slot)))
    ]
    for copy in smalls:
        copy.start()
    lax.fori_loop(0, ROWS, load_row, 0)

    barrier = pltpu.get_barrier_semaphore()

    def greet(i, carry):
        pl.semaphore_signal(barrier, inc=1, device_id={"tile": tile ^ i}, device_id_type=MESH)
        return carry

    lax.fori_loop(1, tiles, greet, 0)
    for e in range(1, levs):
        for q in range(nx):
            to = {"tile": tile ^ (q * row_len), "lev": lev ^ e}
            pl.semaphore_signal(barrier, inc=1, device_id=to, device_id_type=MESH)

    for copy in smalls:
        copy.wait()
    prepare_stencil(idx, wgt, off, blk, wts)

    xf = xs.reshape(OWN, ML, 128)
    vf = vs.reshape(OWN, KL, 128)
    uf = us.reshape(OWN, ML, 128)
    step = OWN // chunks
    gram = None
    for k in range(chunks):
        build_stencil(off, blk, wts, sten, *BUILD[k])
        here = pl.ds(k * step, step)
        pltpu.make_async_copy(xs.at[here], xs.at[here], load_sem.at[k]).wait()
        pltpu.make_async_copy(vs.at[here], vs.at[here], load_sem.at[chunks + k]).wait()
        term = lax.dot_general(
            lanes(xf, k * step, step), lanes(vf, k * step, step),
            (((1,), (1,)), ((), ())), preferred_element_type=F32,
        )
        gram = term if gram is None else gram + term
    same_lev = (iota((ML, KL), 0) & 3) == (iota((ML, KL), 1) & 3)
    gram = jnp.where(same_lev, gram, 0.0)
    fold_m = one_hot((iota((PM, ML), 1) >> 2) == iota((PM, ML), 0))
    fold_k = one_hot((iota((KL, PK), 0) >> 2) == iota((KL, PK), 1))
    folded = sum(dot(fold_m, piece) for piece in split3(gram))
    partial = sum(dot(piece, fold_k) for piece in split3(folded))
    part.reshape(PM, PK)[...] = partial

    pl.semaphore_wait(barrier, tiles - 1 + nx * (levs - 1))

    def ar_stage(k, n, peer, src, dst, mine):
        def send(i, carry):
            to, device = peer(i)
            pltpu.make_async_remote_copy(
                src_ref=src(to), dst_ref=dst.at[mine], send_sem=ar_send.at[k], recv_sem=ar_recv.at[k],
                device_id=device, device_id_type=MESH,
            ).start()
            return carry

        lax.fori_loop(1, n, send, 0)

    def ar_wait(k, n, dst):
        got = dst.at[pl.ds(0, n - 1)]
        pltpu.make_async_copy(got, got, ar_recv.at[k]).wait()

    def add_up(ref, n):
        terms = [ref[i] for i in range(n)]
        while len(terms) > 1:
            terms = [a + b for a, b in zip(terms[::2], terms[1::2])]
        return terms[0]

    def restrict_inputs(first, last):
        cs = slice(first, last)
        matrix = sten[pl.ds(SIDE, OWN), :, cs].reshape(OWN * 128, last - first)
        rx[:, cs] = dot(lanes(xf, 0, OWN), matrix)
        rv[:, cs] = dot(lanes(vf, 0, OWN), matrix).astype(BF)

    ar_stage(0, n1, peer1, lambda to: part.at[to], ra, mine1)
    ra[mine1] = part[mine1]
    build_stencil(off, blk, wts, sten, *BUILD[3])
    ar_wait(0, n1, ra)
    total = add_up(ra, n1)
    sums[0] = total
    ar_stage(1, n2, peer2, lambda to: sums.at[0], rb, mine2)
    rb[mine2] = total
    restrict_inputs(0, 512)
    ar_wait(1, n2, rb)
    total = add_up(rb, n2)
    sums[1] = total
    ar_stage(2, n1, peer1, lambda to: sums.at[1], rc, mine1)
    rc[mine1] = total
    restrict_inputs(512, CELLS)

    spread_m = one_hot((iota((ML, PM), 0) >> 2) == iota((ML, PM), 1))
    spread_k = one_hot((iota((PK, KL), 1) >> 2) == iota((PK, KL), 0))
    slot_row = jnp.broadcast_to(slot[...], (8, MEMBERS)).astype(F32).astype(BF)
    spread_slot = one_hot((iota((MEMBERS, ML), 1) >> 2) == iota((MEMBERS, ML), 0))
    slot_ml = dot(slot_row, spread_slot)[0:1, :].astype(I32)
    out_rows = SLOTS * LEV * 2
    row, col = iota((out_rows, ML), 0), iota((out_rows, ML), 1)
    taken = ((row >> 3) == slot_ml) & (((row >> 1) & 3) == (col & 3))
    select = [one_hot(taken & ((row & 1) == r)) for r in range(2)]

    ar_wait(2, n1, rc)
    projection = rc.reshape(PM, PK)[...]
    eig_row = jnp.concatenate([eig[...], jnp.zeros((1, PK - VECTORS), F32)], axis=1)
    coef = (eig_row * projection / math.sqrt(cells_total)).astype(BF)
    coef = dot(dot(spread_m, coef).astype(BF), spread_k)
    coef = jnp.where(same_lev, coef, 0.0).astype(BF)

    def update(first, count):
        inc = dot(coef, lanes(vf, first, count))
        for i in range(count):
            uf[first + i] = (
                xf[first + i].astype(F32) - inc[:, i * 128 : (i + 1) * 128]
            ).astype(BF)

    def halo_copy(first, dst, k, to):
        return pltpu.make_async_remote_copy(
            src_ref=us.at[pl.ds(first, SIDE)], dst_ref=dst, send_sem=halo_send.at[k],
            recv_sem=halo_recv.at[k], device_id={"tile": to}, device_id_type=MESH,
        )

    to_low = halo_copy(0, hi, 0, lax.rem(tile + tiles - 1, tiles))
    to_high = halo_copy(OWN - SIDE, lo, 1, lax.rem(tile + 1, tiles))
    update(0, SIDE)
    pl.when(tile > 0)(lambda: to_low.start())
    update(OWN - SIDE, SIDE)
    pl.when(tile < tiles - 1)(lambda: to_high.start())
    build_stencil(off, blk, wts, sten, 0, SIDE)
    build_stencil(off, blk, wts, sten, SIDE + OWN, NB)
    rx[...] = rx[...] - dot(coef, rv[...])
    for i in range(2):
        update(SIDE + 18 * i, 18)

    @pl.when(tile == 0)
    def _():
        lo[...] = jnp.zeros_like(lo)

    @pl.when(tile == tiles - 1)
    def _():
        hi[...] = jnp.zeros_like(hi)

    pl.when(tile < tiles - 1)(lambda: to_low.wait_recv())
    pl.when(tile > 0)(lambda: to_high.wait_recv())

    both = jnp.concatenate(
        [lanes(lo.reshape(SIDE, ML, 128), 0, SIDE), lanes(hi.reshape(SIDE, ML, 128), 0, SIDE)], axis=1
    )
    edge = jnp.concatenate(
        [
            sten[pl.ds(0, SIDE)].reshape(SIDE * 128, CELLS),
            sten[pl.ds(SIDE + OWN, SIDE)].reshape(SIDE * 128, CELLS),
        ],
        axis=0,
    )
    res = (rx[...] + dot(both, edge)).astype(BF)

    picked = sum(
        dot(select[r], jnp.concatenate([res[:, k * 128 : k * 128 + 128] for k in range(r, 6, 2)], axis=1))
        for r in range(2)
    ).astype(BF)
    msf = ms.reshape(SLOTS, WAVES, LEV * 2, 128)
    for j in range(WAVES):
        msf[:, j] = picked[:, j * 128 : (j + 1) * 128].reshape(SLOTS, LEV * 2, 128)

    def send(i, carry):
        to = tile ^ far_first(i)
        pltpu.make_async_remote_copy(
            src_ref=ms.at[to], dst_ref=own.at[tile], send_sem=a2a_send, recv_sem=a2a_recv,
            device_id={"tile": to}, device_id_type=MESH,
        ).start()
        return carry

    lax.fori_loop(0, tiles - 1, send, 0)
    keep = pltpu.make_async_copy(ms.at[tile], own.at[tile], self_sem)
    keep.start()

    def store_row(r, carry):
        for c in range(CB):
            pltpu.make_async_copy(us.at[r * CB + c], upd.at[:, r, :, pl.ds(c * 128, 128)], out_sem).start()
        return carry

    lax.fori_loop(0, ROWS, store_row, 0)

    for k, n, dst in ((0, n1, ra), (1, n2, rb), (2, n1, rc)):
        sent = dst.at[pl.ds(0, n - 1)]
        pltpu.make_async_copy(sent, sent, ar_send.at[k]).wait()
    pl.when(tile > 0)(lambda: to_low.wait_send())
    pl.when(tile < tiles - 1)(lambda: to_high.wait_send())
    pltpu.make_async_copy(us, us, out_sem).wait()
    keep.wait()
    if tiles > 1:
        others = ms.at[pl.ds(0, tiles - 1)]
        pltpu.make_async_copy(others, others, a2a_send).wait()
        pltpu.make_async_copy(others, others, a2a_recv).wait()


def deliver(a, b, upd, own, sem):
    copies = [pltpu.make_async_copy(a, upd, sem.at[0])]
    for j in range(WAVES):
        for lev in range(LEV):
            k = 1 + j * LEV + lev
            copies.append(pltpu.make_async_copy(b.at[:, j, lev], own.at[lev, :, j], sem.at[k]))
    for copy in copies:
        copy.start()
    for copy in copies:
        copy.wait()


def shards(anomalies, lanczos, eigen_weight, stencil_index, stencil_weight, member_slot):
    tiles, levs = lax.axis_size("tile"), lax.axis_size("lev")
    grid = (4, 8, 2) if tiles == 64 else (1, 1, tiles)
    n1, n2 = grid[0] * levs, grid[1] * grid[2]
    sh = PM // n1
    total = LEV * ROWS * COLS * tiles * levs
    hbm = pl.BlockSpec(memory_space=pltpu.HBM)
    shapes = (
        jax.ShapeDtypeStruct((MEMBERS, ROWS, LEV, COLS), BF),
        jax.ShapeDtypeStruct((tiles, WAVES, LEV, 2, 128), BF),
    )
    final = (shapes[0], jax.ShapeDtypeStruct((LEV, tiles, WAVES, 2, 128), BF))
    anywhere = pl.BlockSpec(memory_space=pl.ANY)
    updated, owned = pl.pallas_call(
        functools.partial(kernel, tiles, levs, grid, total),
        out_shape=shapes,
        in_specs=[hbm] * 6,
        out_specs=(anywhere, anywhere),
        scratch_shapes=[
            pltpu.VMEM((POINTS, CELLS), I32),
            pltpu.VMEM((POINTS, CELLS), F32),
            pltpu.VMEM((1, VECTORS), F32),
            pltpu.VMEM((1, MEMBERS), I32),
            pltpu.SemaphoreType.DMA((4,)),
            pltpu.VMEM((OWN, MEMBERS, LEV, 128), BF),
            pltpu.VMEM((OWN, VECTORS, LEV, 128), BF),
            pltpu.VMEM((OWN, MEMBERS, LEV, 128), BF),
            pltpu.VMEM((SIDE, MEMBERS, LEV, 128), BF),
            pltpu.VMEM((SIDE, MEMBERS, LEV, 128), BF),
            pltpu.VMEM((NB, 128, CELLS), BF),
            pltpu.VMEM((ML, CELLS), F32),
            pltpu.VMEM((KL, CELLS), BF),
            pltpu.VMEM((POINTS, CELLS), I32),
            pltpu.VMEM((POINTS, CELLS), I32),
            pltpu.VMEM((POINTS, CELLS), F32),
            pltpu.VMEM((n1, sh, PK), F32),
            pltpu.VMEM((n1, sh, PK), F32),
            pltpu.VMEM((n2, sh, PK), F32),
            pltpu.VMEM((n1, sh, PK), F32),
            pltpu.VMEM((2, sh, PK), F32),
            pltpu.VMEM((SLOTS, WAVES, LEV, 2, 128), BF),
            pltpu.SemaphoreType.DMA((6,)),
            pltpu.SemaphoreType.DMA(()),
            pltpu.SemaphoreType.DMA((3,)),
            pltpu.SemaphoreType.DMA((3,)),
            pltpu.SemaphoreType.DMA((2,)),
            pltpu.SemaphoreType.DMA((2,)),
            pltpu.SemaphoreType.DMA(()),
            pltpu.SemaphoreType.DMA(()),
            pltpu.SemaphoreType.DMA(()),
        ],
        compiler_params=pltpu.CompilerParams(
            collective_id=0, has_side_effects=True, vmem_limit_bytes=40 * 2**20
        ),
    )(
        *(
            pltpu.with_memory_space_constraint(a, pltpu.HBM)
            for a in (
                anomalies.transpose(0, 2, 1, 3),
                lanczos.transpose(0, 2, 1, 3),
                stencil_index,
                stencil_weight,
                eigen_weight.reshape(1, -1),
                member_slot.reshape(1, -1),
            )
        )
    )
    updated, owned = pl.pallas_call(
        deliver,
        out_shape=final,
        in_specs=[anywhere, anywhere],
        out_specs=(hbm, hbm),
        scratch_shapes=[pltpu.SemaphoreType.DMA((1 + WAVES * LEV,))],
        compiler_params=pltpu.CompilerParams(vmem_limit_bytes=2**20),
    )(updated, owned)
    return updated.transpose(0, 2, 1, 3), owned.reshape(1, LEV, tiles * 6, 128)


def solution(mesh):
    placed = (
        P(None, "lev", "tile", None),
        P(None, "lev", "tile", None),
        P(),
        P(None, "tile"),
        P(None, "tile"),
        P(),
    )
    return jax.shard_map(
        shards,
        mesh=mesh,
        in_specs=placed,
        out_specs=(P(None, "lev", "tile", None), P("tile", "lev", None, None)),
        check_vma=False,
    )
```

```python
import functools
import math

import jax
import jax.numpy as jnp
from jax import lax
from jax.experimental import pallas as pl
from jax.experimental.pallas import tpu as pltpu
from jax.sharding import PartitionSpec as P

BF = jnp.bfloat16
F32 = jnp.float32
I32 = jnp.int32
MESH = pl.DeviceIdType.MESH

MEMBERS, VECTORS, LEV, ROWS, COLS = 50, 100, 4, 18, 384
POINTS, CELLS = 6, 768
HALO = 3
CB = COLS // 128
OWN = ROWS * CB
SIDE = HALO * CB
NB = OWN + 2 * SIDE
ML, KL = MEMBERS * LEV, VECTORS * LEV
SLOTS = 64
WAVES = 3
BUILD = (9, 17, 21, 25, 63)
EARLY = 512
PM, PK = 64, 128


def iota(shape, dim):
    return lax.broadcasted_iota(I32, shape, dim)


def dot(a, b):
    return lax.dot_general(a, b, (((1,), (0,)), ((), ())), preferred_element_type=F32)


def one_hot(cond):
    return jnp.where(cond, 1.0, 0.0).astype(BF)


def split3(a):
    hi = a.astype(BF)
    rest = a - hi.astype(F32)
    mid = rest.astype(BF)
    return hi, mid, (rest - mid.astype(F32)).astype(BF)


def lanes(ref, first, count):
    return jnp.concatenate([ref[first + i] for i in range(count)], axis=1)


def far_first(i):
    return ((((0x01627354 >> ((i >> 3) * 4)) & 7) << 1) | (((i >> 1) & 3) << 4) | (i & 1)) ^ 49


def prepare_stencil(idx, wgt, off, blk, wts):
    rows = [idx[p : p + 1, :] for p in range(POINTS)]
    weights = [wgt[p : p + 1, :] for p in range(POINTS)]
    for p in range(POINTS):
        moved = None
        for q in range(p + 1, POINTS):
            same = rows[p] == rows[q]
            hit = same if moved is None else same & ~moved
            weights[q] = jnp.where(hit, weights[q] + weights[p], weights[q])
            moved = same if moved is None else moved | same
        block = rows[p] >> 7
        blk[p : p + 1, :] = block if moved is None else jnp.where(moved, -1, block)
        off[p : p + 1, :] = rows[p] & 127
        wts[p : p + 1, :] = weights[p]


def build_stencil(off, blk, wts, sten, first, last, low=0, high=CELLS):
    for c in range(low // 128, high // 128):
        cs = slice(c * 128, (c + 1) * 128)
        weights = [jnp.broadcast_to(wts[p : p + 1, cs], (16, 128)).astype(BF) for p in range(POINTS)]
        places = [(iota((16, 128), 0) + 16 * i).astype(F32).astype(BF) for i in range(8)]
        blocks, offsets = blk[:, cs], off[:, cs]

        def body(b, carry):
            local = jnp.where(blocks == b, offsets, -1).astype(F32)
            here = [jnp.broadcast_to(local[p : p + 1, :], (16, 128)).astype(BF) for p in range(POINTS)]
            for i in range(8):
                value = jnp.zeros((16, 128), BF)
                for p in range(POINTS):
                    value = jnp.where(here[p] == places[i], weights[p], value)
                sten[b, i * 16 : (i + 1) * 16, cs] = value
            return carry

        lax.fori_loop(first, last, body, 0)


def kernel(
    tiles, levs, grid, cells_total,
    x, v, idx_in, wgt_in, eig_in, slot_in,
    upd, own,
    idx, wgt, eig, slot, small_sem, xs, vs, us, lo, hi, sten, rx, rv, off, blk, wts, part, ra, rb, rc, sums, ms,
    load_sem, out_sem, ar_send, ar_recv, halo_send, halo_recv, a2a_send, a2a_recv, self_sem,
):
    tile, lev = lax.axis_index("tile"), lax.axis_index("lev")
    nx, nz, nc = grid
    row_len = nz * nc
    my_x, my_zc = tile // row_len, lax.rem(tile, row_len)
    n1, n2 = nx * levs, nz * nc
    mine1, mine2 = my_x * levs + lev, my_zc
    lev_bits = levs.bit_length() - 1

    def peer1(i):
        to = mine1 ^ i
        return to, {"tile": (to >> lev_bits) * row_len + my_zc, "lev": to & (levs - 1)}

    def peer2(i):
        return mine2 ^ i, {"tile": tile ^ i}

    chunks = 3
    per = ROWS // chunks

    def load_row(r, carry):
        k = r // per
        for c in range(CB):
            cols = pl.ds(c * 128, 128)
            pltpu.make_async_copy(x.at[:, r, :, cols], xs.at[r * CB + c], load_sem.at[k]).start()
            pltpu.make_async_copy(v.at[:, r, :, cols], vs.at[r * CB + c], load_sem.at[chunks + k]).start()
        return carry

    smalls = [
        pltpu.make_async_copy(src, dst, small_sem.at[i])
        for i, (src, dst) in enumerate(((idx_in, idx), (wgt_in, wgt), (eig_in, eig), (slot_in, slot)))
    ]
    for copy in smalls:
        copy.start()
    for r in range(ROWS):
        load_row(r, 0)

    barrier = pltpu.get_barrier_semaphore()

    def greet(i, carry):
        pl.semaphore_signal(barrier, inc=1, device_id={"tile": tile ^ i}, device_id_type=MESH)
        return carry

    for i in range(1, tiles):
        greet(i, 0)
    for e in range(1, levs):
        for q in range(nx):
            to = {"tile": tile ^ (q * row_len), "lev": lev ^ e}
            pl.semaphore_signal(barrier, inc=1, device_id=to, device_id_type=MESH)

    for copy in smalls:
        copy.wait()
    prepare_stencil(idx, wgt, off, blk, wts)

    xf = xs.reshape(OWN, ML, 128)
    vf = vs.reshape(OWN, KL, 128)
    uf = us.reshape(OWN, ML, 128)
    step = OWN // chunks
    gram = None
    for k in range(chunks):
        build_stencil(off, blk, wts, sten, BUILD[k], BUILD[k + 1], 0, EARLY)
        here = pl.ds(k * step, step)
        pltpu.make_async_copy(xs.at[here], xs.at[here], load_sem.at[k]).wait()
        pltpu.make_async_copy(vs.at[here], vs.at[here], load_sem.at[chunks + k]).wait()
        term = lax.dot_general(
            lanes(xf, k * step, step), lanes(vf, k * step, step),
            (((1,), (1,)), ((), ())), preferred_element_type=F32,
        )
        gram = term if gram is None else gram + term
    same_lev = (iota((ML, KL), 0) & 3) == (iota((ML, KL), 1) & 3)
    gram = jnp.where(same_lev, gram, 0.0)
    fold_m = one_hot((iota((PM, ML), 1) >> 2) == iota((PM, ML), 0))
    fold_k = one_hot((iota((KL, PK), 0) >> 2) == iota((KL, PK), 1))
    folded = sum(dot(fold_m, piece) for piece in split3(gram))
    partial = sum(dot(piece, fold_k) for piece in split3(folded))
    part.reshape(PM, PK)[...] = partial

    pl.semaphore_wait(barrier, tiles - 1 + nx * (levs - 1))

    def ar_stage(k, n, peer, src, dst, mine):
        def send(i, carry):
            to, device = peer(i)
            pltpu.make_async_remote_copy(
                src_ref=src(to), dst_ref=dst.at[mine], send_sem=ar_send.at[k], recv_sem=ar_recv.at[k],
                device_id=device, device_id_type=MESH,
            ).start()
            return carry

        for i in range(1, n):
            send(i, 0)

    def ar_wait(k, n, dst):
        got = dst.at[pl.ds(0, n - 1)]
        pltpu.make_async_copy(got, got, ar_recv.at[k]).wait()

    def add_up(ref, n):
        terms = [ref[i] for i in range(n)]
        while len(terms) > 1:
            terms = [a + b for a, b in zip(terms[::2], terms[1::2])]
        return terms[0]

    def restrict_inputs(first, last):
        cs = slice(first, last)
        matrix = sten[pl.ds(SIDE, OWN), :, cs].reshape(OWN * 128, last - first)
        rx[:, cs] = dot(lanes(xf, 0, OWN), matrix)
        rv[:, cs] = dot(lanes(vf, 0, OWN), matrix).astype(BF)

    ar_stage(0, n1, peer1, lambda to: part.at[to], ra, mine1)
    ra[mine1] = part[mine1]
    build_stencil(off, blk, wts, sten, BUILD[3], BUILD[4], 0, EARLY)
    ar_wait(0, n1, ra)
    total = add_up(ra, n1)
    sums[0] = total
    ar_stage(1, n2, peer2, lambda to: sums.at[0], rb, mine2)
    rb[mine2] = total
    restrict_inputs(0, EARLY)
    ar_wait(1, n2, rb)
    total = add_up(rb, n2)
    sums[1] = total
    ar_stage(2, n1, peer1, lambda to: sums.at[1], rc, mine1)
    rc[mine1] = total
    build_stencil(off, blk, wts, sten, SIDE, SIDE + OWN, EARLY, CELLS)
    build_stencil(off, blk, wts, sten, 0, SIDE, 0, EARLY)

    spread_m = one_hot((iota((ML, PM), 0) >> 2) == iota((ML, PM), 1))
    spread_k = one_hot((iota((PK, KL), 1) >> 2) == iota((PK, KL), 0))
    slot_row = jnp.broadcast_to(slot[...], (8, MEMBERS)).astype(F32).astype(BF)
    spread_slot = one_hot((iota((MEMBERS, ML), 1) >> 2) == iota((MEMBERS, ML), 0))
    slot_ml = dot(slot_row, spread_slot)[0:1, :].astype(I32)
    out_rows = SLOTS * LEV * 2
    row, col = iota((out_rows, ML), 0), iota((out_rows, ML), 1)
    taken = ((row >> 3) == slot_ml) & (((row >> 1) & 3) == (col & 3))
    select = [one_hot(taken & ((row & 1) == r)) for r in range(2)]

    ar_wait(2, n1, rc)
    projection = rc.reshape(PM, PK)[...]
    eig_row = jnp.concatenate([eig[...], jnp.zeros((1, PK - VECTORS), F32)], axis=1)
    coef = (eig_row * projection / math.sqrt(cells_total)).astype(BF)
    coef = dot(dot(spread_m, coef).astype(BF), spread_k)
    coef = jnp.where(same_lev, coef, 0.0).astype(BF)

    def update(first, count):
        inc = dot(coef, lanes(vf, first, count))
        for i in range(count):
            uf[first + i] = (
                xf[first + i].astype(F32) - inc[:, i * 128 : (i + 1) * 128]
            ).astype(BF)

    def halo_copy(first, dst, k, to):
        return pltpu.make_async_remote_copy(
            src_ref=us.at[pl.ds(first, SIDE)], dst_ref=dst, send_sem=halo_send.at[k],
            recv_sem=halo_recv.at[k], device_id={"tile": to}, device_id_type=MESH,
        )

    to_low = halo_copy(0, hi, 0, lax.rem(tile + tiles - 1, tiles))
    to_high = halo_copy(OWN - SIDE, lo, 1, lax.rem(tile + 1, tiles))
    update(0, SIDE)
    pl.when(tile > 0)(lambda: to_low.start())
    update(OWN - SIDE, SIDE)
    pl.when(tile < tiles - 1)(lambda: to_high.start())
    restrict_inputs(EARLY, CELLS)
    build_stencil(off, blk, wts, sten, 0, SIDE, EARLY, CELLS)
    build_stencil(off, blk, wts, sten, SIDE + OWN, NB)
    rx[...] = rx[...] - dot(coef, rv[...])

    @pl.when(tile == 0)
    def _():
        lo[...] = jnp.zeros_like(lo)

    @pl.when(tile == tiles - 1)
    def _():
        hi[...] = jnp.zeros_like(hi)

    pl.when(tile < tiles - 1)(lambda: to_low.wait_recv())
    pl.when(tile > 0)(lambda: to_high.wait_recv())

    both = jnp.concatenate(
        [lanes(lo.reshape(SIDE, ML, 128), 0, SIDE), lanes(hi.reshape(SIDE, ML, 128), 0, SIDE)], axis=1
    )
    edge = jnp.concatenate(
        [
            sten[pl.ds(0, SIDE)].reshape(SIDE * 128, CELLS),
            sten[pl.ds(SIDE + OWN, SIDE)].reshape(SIDE * 128, CELLS),
        ],
        axis=0,
    )
    res = (rx[...] + dot(both, edge)).astype(BF)

    picked = sum(
        dot(select[r], jnp.concatenate([res[:, k * 128 : k * 128 + 128] for k in range(r, 6, 2)], axis=1))
        for r in range(2)
    ).astype(BF)
    msf = ms.reshape(SLOTS, WAVES, LEV * 2, 128)
    for j in range(WAVES):
        msf[:, j] = picked[:, j * 128 : (j + 1) * 128].reshape(SLOTS, LEV * 2, 128)

    def send(i, carry):
        to = tile ^ far_first(i)
        pltpu.make_async_remote_copy(
            src_ref=ms.at[to], dst_ref=own.at[tile], send_sem=a2a_send, recv_sem=a2a_recv,
            device_id={"tile": to}, device_id_type=MESH,
        ).start()
        return carry

    for i in range(tiles - 1):
        send(i, 0)
    keep = pltpu.make_async_copy(ms.at[tile], own.at[tile], self_sem)
    keep.start()

    for i in range(2):
        update(SIDE + 18 * i, 18)

    def store_row(r, carry):
        for c in range(CB):
            pltpu.make_async_copy(us.at[r * CB + c], upd.at[:, r, :, pl.ds(c * 128, 128)], out_sem).start()
        return carry

    for r in range(ROWS):
        store_row(r, 0)

    for k, n, dst in ((0, n1, ra), (1, n2, rb), (2, n1, rc)):
        sent = dst.at[pl.ds(0, n - 1)]
        pltpu.make_async_copy(sent, sent, ar_send.at[k]).wait()
    pl.when(tile > 0)(lambda: to_low.wait_send())
    pl.when(tile < tiles - 1)(lambda: to_high.wait_send())
    pltpu.make_async_copy(us, us, out_sem).wait()
    keep.wait()
    if tiles > 1:
        others = ms.at[pl.ds(0, tiles - 1)]
        pltpu.make_async_copy(others, others, a2a_send).wait()
        pltpu.make_async_copy(others, others, a2a_recv).wait()


def deliver(a, b, upd, own, sem):
    copies = [pltpu.make_async_copy(a, upd, sem.at[0])]
    for j in range(WAVES):
        for lev in range(LEV):
            k = 1 + j * LEV + lev
            copies.append(pltpu.make_async_copy(b.at[:, j, lev], own.at[lev, :, j], sem.at[k]))
    for copy in copies:
        copy.start()
    for copy in copies:
        copy.wait()


def shards(anomalies, lanczos, eigen_weight, stencil_index, stencil_weight, member_slot):
    tiles, levs = lax.axis_size("tile"), lax.axis_size("lev")
    grid = (4, 8, 2) if tiles == 64 else (1, 1, tiles)
    n1, n2 = grid[0] * levs, grid[1] * grid[2]
    sh = PM // n1
    total = LEV * ROWS * COLS * tiles * levs
    hbm = pl.BlockSpec(memory_space=pltpu.HBM)
    shapes = (
        jax.ShapeDtypeStruct((MEMBERS, ROWS, LEV, COLS), BF),
        jax.ShapeDtypeStruct((tiles, WAVES, LEV, 2, 128), BF),
    )
    final = (shapes[0], jax.ShapeDtypeStruct((LEV, tiles, WAVES, 2, 128), BF))
    anywhere = pl.BlockSpec(memory_space=pl.ANY)
    updated, owned = pl.pallas_call(
        functools.partial(kernel, tiles, levs, grid, total),
        out_shape=shapes,
        in_specs=[hbm] * 6,
        out_specs=(anywhere, anywhere),
        scratch_shapes=[
            pltpu.VMEM((POINTS, CELLS), I32),
            pltpu.VMEM((POINTS, CELLS), F32),
            pltpu.VMEM((1, VECTORS), F32),
            pltpu.VMEM((1, MEMBERS), I32),
            pltpu.SemaphoreType.DMA((4,)),
            pltpu.VMEM((OWN, MEMBERS, LEV, 128), BF),
            pltpu.VMEM((OWN, VECTORS, LEV, 128), BF),
            pltpu.VMEM((OWN, MEMBERS, LEV, 128), BF),
            pltpu.VMEM((SIDE, MEMBERS, LEV, 128), BF),
            pltpu.VMEM((SIDE, MEMBERS, LEV, 128), BF),
            pltpu.VMEM((NB, 128, CELLS), BF),
            pltpu.VMEM((ML, CELLS), F32),
            pltpu.VMEM((KL, CELLS), BF),
            pltpu.VMEM((POINTS, CELLS), I32),
            pltpu.VMEM((POINTS, CELLS), I32),
            pltpu.VMEM((POINTS, CELLS), F32),
            pltpu.VMEM((n1, sh, PK), F32),
            pltpu.VMEM((n1, sh, PK), F32),
            pltpu.VMEM((n2, sh, PK), F32),
            pltpu.VMEM((n1, sh, PK), F32),
            pltpu.VMEM((2, sh, PK), F32),
            pltpu.VMEM((SLOTS, WAVES, LEV, 2, 128), BF),
            pltpu.SemaphoreType.DMA((6,)),
            pltpu.SemaphoreType.DMA(()),
            pltpu.SemaphoreType.DMA((3,)),
            pltpu.SemaphoreType.DMA((3,)),
            pltpu.SemaphoreType.DMA((2,)),
            pltpu.SemaphoreType.DMA((2,)),
            pltpu.SemaphoreType.DMA(()),
            pltpu.SemaphoreType.DMA(()),
            pltpu.SemaphoreType.DMA(()),
        ],
        compiler_params=pltpu.CompilerParams(
            collective_id=0, has_side_effects=True, vmem_limit_bytes=40 * 2**20
        ),
    )(
        *(
            pltpu.with_memory_space_constraint(a, pltpu.HBM)
            for a in (
                anomalies.transpose(0, 2, 1, 3),
                lanczos.transpose(0, 2, 1, 3),
                stencil_index,
                stencil_weight,
                eigen_weight.reshape(1, -1),
                member_slot.reshape(1, -1),
            )
        )
    )
    updated, owned = pl.pallas_call(
        deliver,
        out_shape=final,
        in_specs=[anywhere, anywhere],
        out_specs=(hbm, hbm),
        scratch_shapes=[pltpu.SemaphoreType.DMA((1 + WAVES * LEV,))],
        compiler_params=pltpu.CompilerParams(vmem_limit_bytes=2**20),
    )(updated, owned)
    return updated.transpose(0, 2, 1, 3), owned.reshape(1, LEV, tiles * 6, 128)


def solution(mesh):
    placed = (
        P(None, "lev", "tile", None),
        P(None, "lev", "tile", None),
        P(),
        P(None, "tile"),
        P(None, "tile"),
        P(),
    )
    return jax.shard_map(
        shards,
        mesh=mesh,
        in_specs=placed,
        out_specs=(P(None, "lev", "tile", None), P("tile", "lev", None, None)),
        check_vma=False,
    )
```

```python
import functools
import math

import jax
import jax.numpy as jnp
from jax import lax
from jax.experimental import pallas as pl
from jax.experimental.pallas import tpu as pltpu
from jax.sharding import PartitionSpec as P

BF = jnp.bfloat16
F32 = jnp.float32
I32 = jnp.int32
MESH = pl.DeviceIdType.MESH

MEMBERS, VECTORS, LEV, ROWS, COLS = 50, 100, 4, 18, 384
POINTS, CELLS = 6, 768
HALO = 3
CB = COLS // 128
OWN = ROWS * CB
SIDE = HALO * CB
NB = OWN + 2 * SIDE
ML, KL = MEMBERS * LEV, VECTORS * LEV
SLOTS = 64
WAVES = 3
BUILD = (9, 18, 23, 28, 63)
EARLY = 512
PM, PK = 64, 128


def iota(shape, dim):
    return lax.broadcasted_iota(I32, shape, dim)


def dot(a, b):
    return lax.dot_general(a, b, (((1,), (0,)), ((), ())), preferred_element_type=F32)


def one_hot(cond):
    return jnp.where(cond, 1.0, 0.0).astype(BF)


def split3(a):
    hi = a.astype(BF)
    rest = a - hi.astype(F32)
    mid = rest.astype(BF)
    return hi, mid, (rest - mid.astype(F32)).astype(BF)


def lanes(ref, first, count):
    return jnp.concatenate([ref[first + i] for i in range(count)], axis=1)


def far_first(i):
    return ((((0x01627354 >> ((i >> 3) * 4)) & 7) << 1) | (((i >> 1) & 3) << 4) | (i & 1)) ^ 49


def prepare_stencil(idx, wgt, off, blk, wts):
    rows = [idx[p : p + 1, :] for p in range(POINTS)]
    weights = [wgt[p : p + 1, :] for p in range(POINTS)]
    for p in range(POINTS):
        moved = None
        for q in range(p + 1, POINTS):
            same = rows[p] == rows[q]
            hit = same if moved is None else same & ~moved
            weights[q] = jnp.where(hit, weights[q] + weights[p], weights[q])
            moved = same if moved is None else moved | same
        block = rows[p] >> 7
        blk[p : p + 1, :] = block if moved is None else jnp.where(moved, -1, block)
        off[p : p + 1, :] = rows[p] & 127
        wts[p : p + 1, :] = weights[p]


def build_stencil(off, blk, wts, sten, first, last, low=0, high=CELLS):
    for c in range(low // 128, high // 128):
        cs = slice(c * 128, (c + 1) * 128)
        weights = [jnp.broadcast_to(wts[p : p + 1, cs], (16, 128)).astype(BF) for p in range(POINTS)]
        places = [(iota((16, 128), 0) + 16 * i).astype(F32).astype(BF) for i in range(8)]
        blocks, offsets = blk[:, cs], off[:, cs]

        def body(b, carry):
            local = jnp.where(blocks == b, offsets, -1).astype(F32)
            here = [jnp.broadcast_to(local[p : p + 1, :], (16, 128)).astype(BF) for p in range(POINTS)]
            for i in range(8):
                value = jnp.zeros((16, 128), BF)
                for p in range(POINTS):
                    value = jnp.where(here[p] == places[i], weights[p], value)
                sten[b, i * 16 : (i + 1) * 16, cs] = value
            return carry

        lax.fori_loop(first, last, body, 0)


def kernel(
    tiles, levs, grid, cells_total,
    x, v, idx_in, wgt_in, eig_in, slot_in,
    upd, own,
    idx, wgt, eig, slot, small_sem, xs, vs, us, lo, hi, sten, rx, rv, off, blk, wts, part, ra, rb, rc, sums, ms,
    load_sem, out_sem, ar_send, ar_recv, halo_send, halo_recv, a2a_send, a2a_recv, self_sem,
):
    tile, lev = lax.axis_index("tile"), lax.axis_index("lev")
    nx, nz, nc = grid
    row_len = nz * nc
    my_x, my_zc = tile // row_len, lax.rem(tile, row_len)
    n1, n2 = nx * levs, nz * nc
    mine1, mine2 = my_x * levs + lev, my_zc
    lev_bits = levs.bit_length() - 1

    def peer1(i):
        to = mine1 ^ i
        return to, {"tile": (to >> lev_bits) * row_len + my_zc, "lev": to & (levs - 1)}

    def peer2(i):
        return mine2 ^ i, {"tile": tile ^ i}

    chunks = 3
    per = ROWS // chunks

    def load_row(r, carry):
        k = r // per
        for c in range(CB):
            cols = pl.ds(c * 128, 128)
            pltpu.make_async_copy(x.at[:, r, :, cols], xs.at[r * CB + c], load_sem.at[k]).start()
            pltpu.make_async_copy(v.at[:, r, :, cols], vs.at[r * CB + c], load_sem.at[chunks + k]).start()
        return carry

    smalls = [
        pltpu.make_async_copy(src, dst, small_sem.at[i])
        for i, (src, dst) in enumerate(((idx_in, idx), (wgt_in, wgt), (eig_in, eig), (slot_in, slot)))
    ]
    for copy in smalls:
        copy.start()
    lax.fori_loop(0, ROWS, load_row, 0)

    barrier = pltpu.get_barrier_semaphore()

    def greet(i, carry):
        pl.semaphore_signal(barrier, inc=1, device_id={"tile": tile ^ i}, device_id_type=MESH)
        return carry

    lax.fori_loop(1, tiles, greet, 0)
    for e in range(1, levs):
        for q in range(nx):
            to = {"tile": tile ^ (q * row_len), "lev": lev ^ e}
            pl.semaphore_signal(barrier, inc=1, device_id=to, device_id_type=MESH)

    for copy in smalls:
        copy.wait()
    prepare_stencil(idx, wgt, off, blk, wts)

    xf = xs.reshape(OWN, ML, 128)
    vf = vs.reshape(OWN, KL, 128)
    uf = us.reshape(OWN, ML, 128)
    step = OWN // chunks
    gram = None
    for k in range(chunks):
        build_stencil(off, blk, wts, sten, BUILD[k], BUILD[k + 1], 0, EARLY)
        here = pl.ds(k * step, step)
        pltpu.make_async_copy(xs.at[here], xs.at[here], load_sem.at[k]).wait()
        pltpu.make_async_copy(vs.at[here], vs.at[here], load_sem.at[chunks + k]).wait()
        term = lax.dot_general(
            lanes(xf, k * step, step), lanes(vf, k * step, step),
            (((1,), (1,)), ((), ())), preferred_element_type=F32,
        )
        gram = term if gram is None else gram + term
    same_lev = (iota((ML, KL), 0) & 3) == (iota((ML, KL), 1) & 3)
    gram = jnp.where(same_lev, gram, 0.0)
    fold_m = one_hot((iota((PM, ML), 1) >> 2) == iota((PM, ML), 0))
    fold_k = one_hot((iota((KL, PK), 0) >> 2) == iota((KL, PK), 1))
    folded = sum(dot(fold_m, piece) for piece in split3(gram))
    partial = sum(dot(piece, fold_k) for piece in split3(folded))
    part.reshape(PM, PK)[...] = partial

    pl.semaphore_wait(barrier, tiles - 1 + nx * (levs - 1))

    def ar_stage(k, n, peer, src, dst, mine):
        def send(i, carry):
            to, device = peer(i)
            pltpu.make_async_remote_copy(
                src_ref=src(to), dst_ref=dst.at[mine], send_sem=ar_send.at[k], recv_sem=ar_recv.at[k],
                device_id=device, device_id_type=MESH,
            ).start()
            return carry

        lax.fori_loop(1, n, send, 0)

    def ar_wait(k, n, dst):
        got = dst.at[pl.ds(0, n - 1)]
        pltpu.make_async_copy(got, got, ar_recv.at[k]).wait()

    def add_up(ref, n):
        terms = [ref[i] for i in range(n)]
        while len(terms) > 1:
            terms = [a + b for a, b in zip(terms[::2], terms[1::2])]
        return terms[0]

    def restrict_inputs(first, last):
        cs = slice(first, last)
        matrix = sten[pl.ds(SIDE, OWN), :, cs].reshape(OWN * 128, last - first)
        rx[:, cs] = dot(lanes(xf, 0, OWN), matrix)
        rv[:, cs] = dot(lanes(vf, 0, OWN), matrix).astype(BF)

    ar_stage(0, n1, peer1, lambda to: part.at[to], ra, mine1)
    ra[mine1] = part[mine1]
    build_stencil(off, blk, wts, sten, BUILD[3], BUILD[4], 0, EARLY)
    ar_wait(0, n1, ra)
    total = add_up(ra, n1)
    sums[0] = total
    ar_stage(1, n2, peer2, lambda to: sums.at[0], rb, mine2)
    rb[mine2] = total
    restrict_inputs(0, EARLY)
    ar_wait(1, n2, rb)
    total = add_up(rb, n2)
    sums[1] = total
    ar_stage(2, n1, peer1, lambda to: sums.at[1], rc, mine1)
    rc[mine1] = total
    build_stencil(off, blk, wts, sten, SIDE, SIDE + OWN, EARLY, CELLS)
    restrict_inputs(EARLY, CELLS)

    spread_m = one_hot((iota((ML, PM), 0) >> 2) == iota((ML, PM), 1))
    spread_k = one_hot((iota((PK, KL), 1) >> 2) == iota((PK, KL), 0))
    slot_row = jnp.broadcast_to(slot[...], (8, MEMBERS)).astype(F32).astype(BF)
    spread_slot = one_hot((iota((MEMBERS, ML), 1) >> 2) == iota((MEMBERS, ML), 0))
    slot_ml = dot(slot_row, spread_slot)[0:1, :].astype(I32)
    out_rows = SLOTS * LEV * 2
    row, col = iota((out_rows, ML), 0), iota((out_rows, ML), 1)
    taken = ((row >> 3) == slot_ml) & (((row >> 1) & 3) == (col & 3))
    select = [one_hot(taken & ((row & 1) == r)) for r in range(2)]

    ar_wait(2, n1, rc)
    projection = rc.reshape(PM, PK)[...]
    eig_row = jnp.concatenate([eig[...], jnp.zeros((1, PK - VECTORS), F32)], axis=1)
    coef = (eig_row * projection / math.sqrt(cells_total)).astype(BF)
    coef = dot(dot(spread_m, coef).astype(BF), spread_k)
    coef = jnp.where(same_lev, coef, 0.0).astype(BF)

    def update(first, count):
        inc = dot(coef, lanes(vf, first, count))
        for i in range(count):
            uf[first + i] = (
                xf[first + i].astype(F32) - inc[:, i * 128 : (i + 1) * 128]
            ).astype(BF)

    def halo_copy(first, dst, k, to):
        return pltpu.make_async_remote_copy(
            src_ref=us.at[pl.ds(first, SIDE)], dst_ref=dst, send_sem=halo_send.at[k],
            recv_sem=halo_recv.at[k], device_id={"tile": to}, device_id_type=MESH,
        )

    to_low = halo_copy(0, hi, 0, lax.rem(tile + tiles - 1, tiles))
    to_high = halo_copy(OWN - SIDE, lo, 1, lax.rem(tile + 1, tiles))
    update(0, SIDE)
    pl.when(tile > 0)(lambda: to_low.start())
    update(OWN - SIDE, SIDE)
    pl.when(tile < tiles - 1)(lambda: to_high.start())
    build_stencil(off, blk, wts, sten, 0, SIDE)
    build_stencil(off, blk, wts, sten, SIDE + OWN, NB)
    rx[...] = rx[...] - dot(coef, rv[...])

    @pl.when(tile == 0)
    def _():
        lo[...] = jnp.zeros_like(lo)

    @pl.when(tile == tiles - 1)
    def _():
        hi[...] = jnp.zeros_like(hi)

    pl.when(tile < tiles - 1)(lambda: to_low.wait_recv())
    pl.when(tile > 0)(lambda: to_high.wait_recv())

    both = jnp.concatenate(
        [lanes(lo.reshape(SIDE, ML, 128), 0, SIDE), lanes(hi.reshape(SIDE, ML, 128), 0, SIDE)], axis=1
    )
    edge = jnp.concatenate(
        [
            sten[pl.ds(0, SIDE)].reshape(SIDE * 128, CELLS),
            sten[pl.ds(SIDE + OWN, SIDE)].reshape(SIDE * 128, CELLS),
        ],
        axis=0,
    )
    res = (rx[...] + dot(both, edge)).astype(BF)

    picked = sum(
        dot(select[r], jnp.concatenate([res[:, k * 128 : k * 128 + 128] for k in range(r, 6, 2)], axis=1))
        for r in range(2)
    ).astype(BF)
    msf = ms.reshape(SLOTS, WAVES, LEV * 2, 128)
    for j in range(WAVES):
        msf[:, j] = picked[:, j * 128 : (j + 1) * 128].reshape(SLOTS, LEV * 2, 128)

    def send(i, carry):
        to = tile ^ far_first(i)
        pltpu.make_async_remote_copy(
            src_ref=ms.at[to], dst_ref=own.at[tile], send_sem=a2a_send, recv_sem=a2a_recv,
            device_id={"tile": to}, device_id_type=MESH,
        ).start()
        return carry

    for i in range(tiles - 1):
        send(i, 0)
    keep = pltpu.make_async_copy(ms.at[tile], own.at[tile], self_sem)
    keep.start()

    for i in range(2):
        update(SIDE + 18 * i, 18)

    def store_row(r, carry):
        for c in range(CB):
            pltpu.make_async_copy(us.at[r * CB + c], upd.at[:, r, :, pl.ds(c * 128, 128)], out_sem).start()
        return carry

    lax.fori_loop(0, ROWS, store_row, 0)

    for k, n, dst in ((0, n1, ra), (1, n2, rb), (2, n1, rc)):
        sent = dst.at[pl.ds(0, n - 1)]
        pltpu.make_async_copy(sent, sent, ar_send.at[k]).wait()
    pl.when(tile > 0)(lambda: to_low.wait_send())
    pl.when(tile < tiles - 1)(lambda: to_high.wait_send())
    pltpu.make_async_copy(us, us, out_sem).wait()
    keep.wait()
    if tiles > 1:
        others = ms.at[pl.ds(0, tiles - 1)]
        pltpu.make_async_copy(others, others, a2a_send).wait()
        pltpu.make_async_copy(others, others, a2a_recv).wait()


def deliver(a, b, upd, own, sem):
    copies = [pltpu.make_async_copy(a, upd, sem.at[0])]
    for j in range(WAVES):
        for lev in range(LEV):
            k = 1 + j * LEV + lev
            copies.append(pltpu.make_async_copy(b.at[:, j, lev], own.at[lev, :, j], sem.at[k]))
    for copy in copies:
        copy.start()
    for copy in copies:
        copy.wait()


def shards(anomalies, lanczos, eigen_weight, stencil_index, stencil_weight, member_slot):
    tiles, levs = lax.axis_size("tile"), lax.axis_size("lev")
    grid = (4, 8, 2) if tiles == 64 else (1, 1, tiles)
    n1, n2 = grid[0] * levs, grid[1] * grid[2]
    sh = PM // n1
    total = LEV * ROWS * COLS * tiles * levs
    hbm = pl.BlockSpec(memory_space=pltpu.HBM)
    shapes = (
        jax.ShapeDtypeStruct((MEMBERS, ROWS, LEV, COLS), BF),
        jax.ShapeDtypeStruct((tiles, WAVES, LEV, 2, 128), BF),
    )
    final = (shapes[0], jax.ShapeDtypeStruct((LEV, tiles, WAVES, 2, 128), BF))
    anywhere = pl.BlockSpec(memory_space=pl.ANY)
    updated, owned = pl.pallas_call(
        functools.partial(kernel, tiles, levs, grid, total),
        out_shape=shapes,
        in_specs=[hbm] * 6,
        out_specs=(anywhere, anywhere),
        scratch_shapes=[
            pltpu.VMEM((POINTS, CELLS), I32),
            pltpu.VMEM((POINTS, CELLS), F32),
            pltpu.VMEM((1, VECTORS), F32),
            pltpu.VMEM((1, MEMBERS), I32),
            pltpu.SemaphoreType.DMA((4,)),
            pltpu.VMEM((OWN, MEMBERS, LEV, 128), BF),
            pltpu.VMEM((OWN, VECTORS, LEV, 128), BF),
            pltpu.VMEM((OWN, MEMBERS, LEV, 128), BF),
            pltpu.VMEM((SIDE, MEMBERS, LEV, 128), BF),
            pltpu.VMEM((SIDE, MEMBERS, LEV, 128), BF),
            pltpu.VMEM((NB, 128, CELLS), BF),
            pltpu.VMEM((ML, CELLS), F32),
            pltpu.VMEM((KL, CELLS), BF),
            pltpu.VMEM((POINTS, CELLS), I32),
            pltpu.VMEM((POINTS, CELLS), I32),
            pltpu.VMEM((POINTS, CELLS), F32),
            pltpu.VMEM((n1, sh, PK), F32),
            pltpu.VMEM((n1, sh, PK), F32),
            pltpu.VMEM((n2, sh, PK), F32),
            pltpu.VMEM((n1, sh, PK), F32),
            pltpu.VMEM((2, sh, PK), F32),
            pltpu.VMEM((SLOTS, WAVES, LEV, 2, 128), BF),
            pltpu.SemaphoreType.DMA((6,)),
            pltpu.SemaphoreType.DMA(()),
            pltpu.SemaphoreType.DMA((3,)),
            pltpu.SemaphoreType.DMA((3,)),
            pltpu.SemaphoreType.DMA((2,)),
            pltpu.SemaphoreType.DMA((2,)),
            pltpu.SemaphoreType.DMA(()),
            pltpu.SemaphoreType.DMA(()),
            pltpu.SemaphoreType.DMA(()),
        ],
        compiler_params=pltpu.CompilerParams(
            collective_id=0, has_side_effects=True, vmem_limit_bytes=40 * 2**20
        ),
    )(
        *(
            pltpu.with_memory_space_constraint(a, pltpu.HBM)
            for a in (
                anomalies.transpose(0, 2, 1, 3),
                lanczos.transpose(0, 2, 1, 3),
                stencil_index,
                stencil_weight,
                eigen_weight.reshape(1, -1),
                member_slot.reshape(1, -1),
            )
        )
    )
    updated, owned = pl.pallas_call(
        deliver,
        out_shape=final,
        in_specs=[anywhere, anywhere],
        out_specs=(hbm, hbm),
        scratch_shapes=[pltpu.SemaphoreType.DMA((1 + WAVES * LEV,))],
        compiler_params=pltpu.CompilerParams(vmem_limit_bytes=2**20),
    )(updated, owned)
    return updated.transpose(0, 2, 1, 3), owned.reshape(1, LEV, tiles * 6, 128)


def solution(mesh):
    placed = (
        P(None, "lev", "tile", None),
        P(None, "lev", "tile", None),
        P(),
        P(None, "tile"),
        P(None, "tile"),
        P(),
    )
    return jax.shard_map(
        shards,
        mesh=mesh,
        in_specs=placed,
        out_specs=(P(None, "lev", "tile", None), P("tile", "lev", None, None)),
        check_vma=False,
    )
```

```python
import functools
import math

import jax
import jax.numpy as jnp
from jax import lax
from jax.experimental import pallas as pl
from jax.experimental.pallas import tpu as pltpu
from jax.sharding import PartitionSpec as P

BF = jnp.bfloat16
F32 = jnp.float32
I32 = jnp.int32
MESH = pl.DeviceIdType.MESH

MEMBERS, VECTORS, LEV, ROWS, COLS = 50, 100, 4, 18, 384
POINTS, CELLS = 6, 768
HALO = 3
CB = COLS // 128
OWN = ROWS * CB
SIDE = HALO * CB
NB = OWN + 2 * SIDE
ML, KL = MEMBERS * LEV, VECTORS * LEV
SLOTS = 64
WAVES = 3
BUILD = (9, 18, 23, 28, 63)
EARLY = 512
PM, PK = 64, 128


def iota(shape, dim):
    return lax.broadcasted_iota(I32, shape, dim)


def dot(a, b):
    return lax.dot_general(a, b, (((1,), (0,)), ((), ())), preferred_element_type=F32)


def one_hot(cond):
    return jnp.where(cond, 1.0, 0.0).astype(BF)


def split3(a):
    hi = a.astype(BF)
    rest = a - hi.astype(F32)
    mid = rest.astype(BF)
    return hi, mid, (rest - mid.astype(F32)).astype(BF)


def lanes(ref, first, count):
    return jnp.concatenate([ref[first + i] for i in range(count)], axis=1)


def far_first(i):
    return ((((0x01627354 >> ((i >> 3) * 4)) & 7) << 1) | (((i >> 1) & 3) << 4) | (i & 1)) ^ 49


def prepare_stencil(idx, wgt, off, blk, wts):
    rows = [idx[p : p + 1, :] for p in range(POINTS)]
    weights = [wgt[p : p + 1, :] for p in range(POINTS)]
    for p in range(POINTS):
        moved = None
        for q in range(p + 1, POINTS):
            same = rows[p] == rows[q]
            hit = same if moved is None else same & ~moved
            weights[q] = jnp.where(hit, weights[q] + weights[p], weights[q])
            moved = same if moved is None else moved | same
        block = rows[p] >> 7
        blk[p : p + 1, :] = block if moved is None else jnp.where(moved, -1, block)
        off[p : p + 1, :] = rows[p] & 127
        wts[p : p + 1, :] = weights[p]


def build_stencil(off, blk, wts, sten, first, last, low=0, high=CELLS):
    for c in range(low // 128, high // 128):
        cs = slice(c * 128, (c + 1) * 128)
        weights = [jnp.broadcast_to(wts[p : p + 1, cs], (16, 128)).astype(BF) for p in range(POINTS)]
        places = [(iota((16, 128), 0) + 16 * i).astype(F32).astype(BF) for i in range(8)]
        blocks, offsets = blk[:, cs], off[:, cs]

        def body(b, carry):
            local = jnp.where(blocks == b, offsets, -1).astype(F32)
            here = [jnp.broadcast_to(local[p : p + 1, :], (16, 128)).astype(BF) for p in range(POINTS)]
            for i in range(8):
                value = jnp.zeros((16, 128), BF)
                for p in range(POINTS):
                    value = jnp.where(here[p] == places[i], weights[p], value)
                sten[b, i * 16 : (i + 1) * 16, cs] = value
            return carry

        lax.fori_loop(first, last, body, 0)


def kernel(
    tiles, levs, grid, cells_total,
    x, v, idx_in, wgt_in, eig_in, slot_in,
    upd, own,
    idx, wgt, eig, slot, small_sem, xs, vs, us, lo, hi, sten, rx, rv, off, blk, wts, part, ra, rb, rc, sums, ms,
    load_sem, out_sem, ar_send, ar_recv, halo_send, halo_recv, a2a_send, a2a_recv, self_sem,
):
    tile, lev = lax.axis_index("tile"), lax.axis_index("lev")
    nx, nz, nc = grid
    row_len = nz * nc
    my_x, my_zc = tile // row_len, lax.rem(tile, row_len)
    n1, n2 = nx * levs, nz * nc
    mine1, mine2 = my_x * levs + lev, my_zc
    lev_bits = levs.bit_length() - 1

    def peer1(i):
        to = mine1 ^ i
        return to, {"tile": (to >> lev_bits) * row_len + my_zc, "lev": to & (levs - 1)}

    def peer2(i):
        return mine2 ^ i, {"tile": tile ^ i}

    chunks = 3
    per = ROWS // chunks

    def load_row(r, carry):
        k = r // per
        for c in range(CB):
            cols = pl.ds(c * 128, 128)
            pltpu.make_async_copy(x.at[:, r, :, cols], xs.at[r * CB + c], load_sem.at[k]).start()
            pltpu.make_async_copy(v.at[:, r, :, cols], vs.at[r * CB + c], load_sem.at[chunks + k]).start()
        return carry

    smalls = [
        pltpu.make_async_copy(src, dst, small_sem.at[i])
        for i, (src, dst) in enumerate(((idx_in, idx), (wgt_in, wgt), (eig_in, eig), (slot_in, slot)))
    ]
    for copy in smalls:
        copy.start()
    lax.fori_loop(0, per, load_row, 0)

    barrier = pltpu.get_barrier_semaphore()

    def greet(i, carry):
        pl.semaphore_signal(
            barrier, inc=1, device_id={"tile": tile ^ far_first(i)}, device_id_type=MESH
        )
        return carry

    far = min(24, tiles - 1)
    lax.fori_loop(0, far, greet, 0)
    for e in range(1, levs):
        for q in range(nx):
            to = {"tile": tile ^ (q * row_len), "lev": lev ^ e}
            pl.semaphore_signal(barrier, inc=1, device_id=to, device_id_type=MESH)
    lax.fori_loop(per, ROWS, load_row, 0)
    lax.fori_loop(far, tiles - 1, greet, 0)

    for copy in smalls:
        copy.wait()
    prepare_stencil(idx, wgt, off, blk, wts)

    xf = xs.reshape(OWN, ML, 128)
    vf = vs.reshape(OWN, KL, 128)
    uf = us.reshape(OWN, ML, 128)
    step = OWN // chunks
    gram = None
    for k in range(chunks):
        build_stencil(off, blk, wts, sten, BUILD[k], BUILD[k + 1], 0, EARLY)
        here = pl.ds(k * step, step)
        pltpu.make_async_copy(xs.at[here], xs.at[here], load_sem.at[k]).wait()
        pltpu.make_async_copy(vs.at[here], vs.at[here], load_sem.at[chunks + k]).wait()
        term = lax.dot_general(
            lanes(xf, k * step, step), lanes(vf, k * step, step),
            (((1,), (1,)), ((), ())), preferred_element_type=F32,
        )
        gram = term if gram is None else gram + term
    same_lev = (iota((ML, KL), 0) & 3) == (iota((ML, KL), 1) & 3)
    gram = jnp.where(same_lev, gram, 0.0)
    fold_m = one_hot((iota((PM, ML), 1) >> 2) == iota((PM, ML), 0))
    fold_k = one_hot((iota((KL, PK), 0) >> 2) == iota((KL, PK), 1))
    folded = sum(dot(fold_m, piece) for piece in split3(gram))
    partial = sum(dot(piece, fold_k) for piece in split3(folded))
    part.reshape(PM, PK)[...] = partial

    pl.semaphore_wait(barrier, tiles - 1 + nx * (levs - 1))

    def ar_stage(k, n, peer, src, dst, mine):
        def send(i, carry):
            to, device = peer(i)
            pltpu.make_async_remote_copy(
                src_ref=src(to), dst_ref=dst.at[mine], send_sem=ar_send.at[k], recv_sem=ar_recv.at[k],
                device_id=device, device_id_type=MESH,
            ).start()
            return carry

        lax.fori_loop(1, n, send, 0)

    def ar_wait(k, n, dst):
        got = dst.at[pl.ds(0, n - 1)]
        pltpu.make_async_copy(got, got, ar_recv.at[k]).wait()

    def add_up(ref, n):
        terms = [ref[i] for i in range(n)]
        while len(terms) > 1:
            terms = [a + b for a, b in zip(terms[::2], terms[1::2])]
        return terms[0]

    def restrict_inputs(first, last):
        cs = slice(first, last)
        matrix = sten[pl.ds(SIDE, OWN), :, cs].reshape(OWN * 128, last - first)
        rx[:, cs] = dot(lanes(xf, 0, OWN), matrix)
        rv[:, cs] = dot(lanes(vf, 0, OWN), matrix).astype(BF)

    ar_stage(0, n1, peer1, lambda to: part.at[to], ra, mine1)
    ra[mine1] = part[mine1]
    build_stencil(off, blk, wts, sten, BUILD[3], BUILD[4], 0, EARLY)
    ar_wait(0, n1, ra)
    total = add_up(ra, n1)
    sums[0] = total
    ar_stage(1, n2, peer2, lambda to: sums.at[0], rb, mine2)
    rb[mine2] = total
    restrict_inputs(0, EARLY)
    ar_wait(1, n2, rb)
    total = add_up(rb, n2)
    sums[1] = total
    ar_stage(2, n1, peer1, lambda to: sums.at[1], rc, mine1)
    rc[mine1] = total
    build_stencil(off, blk, wts, sten, SIDE, SIDE + OWN, EARLY, CELLS)
    restrict_inputs(EARLY, CELLS)

    spread_m = one_hot((iota((ML, PM), 0) >> 2) == iota((ML, PM), 1))
    spread_k = one_hot((iota((PK, KL), 1) >> 2) == iota((PK, KL), 0))
    slot_row = jnp.broadcast_to(slot[...], (8, MEMBERS)).astype(F32).astype(BF)
    spread_slot = one_hot((iota((MEMBERS, ML), 1) >> 2) == iota((MEMBERS, ML), 0))
    slot_ml = dot(slot_row, spread_slot)[0:1, :].astype(I32)
    out_rows = SLOTS * LEV * 2
    row, col = iota((out_rows, ML), 0), iota((out_rows, ML), 1)
    taken = ((row >> 3) == slot_ml) & (((row >> 1) & 3) == (col & 3))
    select = [one_hot(taken & ((row & 1) == r)) for r in range(2)]

    ar_wait(2, n1, rc)
    projection = rc.reshape(PM, PK)[...]
    eig_row = jnp.concatenate([eig[...], jnp.zeros((1, PK - VECTORS), F32)], axis=1)
    coef = (eig_row * projection / math.sqrt(cells_total)).astype(BF)
    coef = dot(dot(spread_m, coef).astype(BF), spread_k)
    coef = jnp.where(same_lev, coef, 0.0).astype(BF)

    def update(first, count):
        inc = dot(coef, lanes(vf, first, count))
        for i in range(count):
            uf[first + i] = (
                xf[first + i].astype(F32) - inc[:, i * 128 : (i + 1) * 128]
            ).astype(BF)

    def halo_copy(first, dst, k, to):
        return pltpu.make_async_remote_copy(
            src_ref=us.at[pl.ds(first, SIDE)], dst_ref=dst, send_sem=halo_send.at[k],
            recv_sem=halo_recv.at[k], device_id={"tile": to}, device_id_type=MESH,
        )

    to_low = halo_copy(0, hi, 0, lax.rem(tile + tiles - 1, tiles))
    to_high = halo_copy(OWN - SIDE, lo, 1, lax.rem(tile + 1, tiles))
    update(0, SIDE)
    pl.when(tile > 0)(lambda: to_low.start())
    update(OWN - SIDE, SIDE)
    pl.when(tile < tiles - 1)(lambda: to_high.start())
    build_stencil(off, blk, wts, sten, 0, SIDE)
    build_stencil(off, blk, wts, sten, SIDE + OWN, NB)
    rx[...] = rx[...] - dot(coef, rv[...])

    @pl.when(tile == 0)
    def _():
        lo[...] = jnp.zeros_like(lo)

    @pl.when(tile == tiles - 1)
    def _():
        hi[...] = jnp.zeros_like(hi)

    pl.when(tile < tiles - 1)(lambda: to_low.wait_recv())
    pl.when(tile > 0)(lambda: to_high.wait_recv())

    both = jnp.concatenate(
        [lanes(lo.reshape(SIDE, ML, 128), 0, SIDE), lanes(hi.reshape(SIDE, ML, 128), 0, SIDE)], axis=1
    )
    edge = jnp.concatenate(
        [
            sten[pl.ds(0, SIDE)].reshape(SIDE * 128, CELLS),
            sten[pl.ds(SIDE + OWN, SIDE)].reshape(SIDE * 128, CELLS),
        ],
        axis=0,
    )
    res = (rx[...] + dot(both, edge)).astype(BF)

    picked = sum(
        dot(select[r], jnp.concatenate([res[:, k * 128 : k * 128 + 128] for k in range(r, 6, 2)], axis=1))
        for r in range(2)
    ).astype(BF)
    msf = ms.reshape(SLOTS, WAVES, LEV * 2, 128)
    for j in range(WAVES):
        msf[:, j] = picked[:, j * 128 : (j + 1) * 128].reshape(SLOTS, LEV * 2, 128)

    def send(i, carry):
        to = tile ^ far_first(i)
        pltpu.make_async_remote_copy(
            src_ref=ms.at[to], dst_ref=own.at[tile], send_sem=a2a_send, recv_sem=a2a_recv,
            device_id={"tile": to}, device_id_type=MESH,
        ).start()
        return carry

    for i in range(tiles - 1):
        send(i, 0)
    keep = pltpu.make_async_copy(ms.at[tile], own.at[tile], self_sem)
    keep.start()

    for i in range(2):
        update(SIDE + 18 * i, 18)

    def store_row(r, carry):
        for c in range(CB):
            pltpu.make_async_copy(us.at[r * CB + c], upd.at[:, r, :, pl.ds(c * 128, 128)], out_sem).start()
        return carry

    lax.fori_loop(0, ROWS, store_row, 0)

    for k, n, dst in ((0, n1, ra), (1, n2, rb), (2, n1, rc)):
        sent = dst.at[pl.ds(0, n - 1)]
        pltpu.make_async_copy(sent, sent, ar_send.at[k]).wait()
    pl.when(tile > 0)(lambda: to_low.wait_send())
    pl.when(tile < tiles - 1)(lambda: to_high.wait_send())
    pltpu.make_async_copy(us, us, out_sem).wait()
    keep.wait()
    if tiles > 1:
        others = ms.at[pl.ds(0, tiles - 1)]
        pltpu.make_async_copy(others, others, a2a_send).wait()
        pltpu.make_async_copy(others, others, a2a_recv).wait()


def deliver(a, b, upd, own, sem):
    copies = [pltpu.make_async_copy(a, upd, sem.at[0])]
    for j in range(WAVES):
        for lev in range(LEV):
            k = 1 + j * LEV + lev
            copies.append(pltpu.make_async_copy(b.at[:, j, lev], own.at[lev, :, j], sem.at[k]))
    for copy in copies:
        copy.start()
    for copy in copies:
        copy.wait()


def shards(anomalies, lanczos, eigen_weight, stencil_index, stencil_weight, member_slot):
    tiles, levs = lax.axis_size("tile"), lax.axis_size("lev")
    grid = (4, 8, 2) if tiles == 64 else (1, 1, tiles)
    n1, n2 = grid[0] * levs, grid[1] * grid[2]
    sh = PM // n1
    total = LEV * ROWS * COLS * tiles * levs
    hbm = pl.BlockSpec(memory_space=pltpu.HBM)
    shapes = (
        jax.ShapeDtypeStruct((MEMBERS, ROWS, LEV, COLS), BF),
        jax.ShapeDtypeStruct((tiles, WAVES, LEV, 2, 128), BF),
    )
    final = (shapes[0], jax.ShapeDtypeStruct((LEV, tiles, WAVES, 2, 128), BF))
    anywhere = pl.BlockSpec(memory_space=pl.ANY)
    updated, owned = pl.pallas_call(
        functools.partial(kernel, tiles, levs, grid, total),
        out_shape=shapes,
        in_specs=[hbm] * 6,
        out_specs=(anywhere, anywhere),
        scratch_shapes=[
            pltpu.VMEM((POINTS, CELLS), I32),
            pltpu.VMEM((POINTS, CELLS), F32),
            pltpu.VMEM((1, VECTORS), F32),
            pltpu.VMEM((1, MEMBERS), I32),
            pltpu.SemaphoreType.DMA((4,)),
            pltpu.VMEM((OWN, MEMBERS, LEV, 128), BF),
            pltpu.VMEM((OWN, VECTORS, LEV, 128), BF),
            pltpu.VMEM((OWN, MEMBERS, LEV, 128), BF),
            pltpu.VMEM((SIDE, MEMBERS, LEV, 128), BF),
            pltpu.VMEM((SIDE, MEMBERS, LEV, 128), BF),
            pltpu.VMEM((NB, 128, CELLS), BF),
            pltpu.VMEM((ML, CELLS), F32),
            pltpu.VMEM((KL, CELLS), BF),
            pltpu.VMEM((POINTS, CELLS), I32),
            pltpu.VMEM((POINTS, CELLS), I32),
            pltpu.VMEM((POINTS, CELLS), F32),
            pltpu.VMEM((n1, sh, PK), F32),
            pltpu.VMEM((n1, sh, PK), F32),
            pltpu.VMEM((n2, sh, PK), F32),
            pltpu.VMEM((n1, sh, PK), F32),
            pltpu.VMEM((2, sh, PK), F32),
            pltpu.VMEM((SLOTS, WAVES, LEV, 2, 128), BF),
            pltpu.SemaphoreType.DMA((6,)),
            pltpu.SemaphoreType.DMA(()),
            pltpu.SemaphoreType.DMA((3,)),
            pltpu.SemaphoreType.DMA((3,)),
            pltpu.SemaphoreType.DMA((2,)),
            pltpu.SemaphoreType.DMA((2,)),
            pltpu.SemaphoreType.DMA(()),
            pltpu.SemaphoreType.DMA(()),
            pltpu.SemaphoreType.DMA(()),
        ],
        compiler_params=pltpu.CompilerParams(
            collective_id=0, has_side_effects=True, vmem_limit_bytes=40 * 2**20
        ),
    )(
        *(
            pltpu.with_memory_space_constraint(a, pltpu.HBM)
            for a in (
                anomalies.transpose(0, 2, 1, 3),
                lanczos.transpose(0, 2, 1, 3),
                stencil_index,
                stencil_weight,
                eigen_weight.reshape(1, -1),
                member_slot.reshape(1, -1),
            )
        )
    )
    updated, owned = pl.pallas_call(
        deliver,
        out_shape=final,
        in_specs=[anywhere, anywhere],
        out_specs=(hbm, hbm),
        scratch_shapes=[pltpu.SemaphoreType.DMA((1 + WAVES * LEV,))],
        compiler_params=pltpu.CompilerParams(vmem_limit_bytes=2**20),
    )(updated, owned)
    return updated.transpose(0, 2, 1, 3), owned.reshape(1, LEV, tiles * 6, 128)


def solution(mesh):
    placed = (
        P(None, "lev", "tile", None),
        P(None, "lev", "tile", None),
        P(),
        P(None, "tile"),
        P(None, "tile"),
        P(),
    )
    return jax.shard_map(
        shards,
        mesh=mesh,
        in_specs=placed,
        out_specs=(P(None, "lev", "tile", None), P("tile", "lev", None, None)),
        check_vma=False,
    )
```
